256 devices in a mesh: rows: 64 (over x, z, core), cols: 4 (over y).
Axes of the slice: x: 4, y: 4, z: 8, core: 2. Of those that a mesh axis runs over, the one named last changes fastest.
Arguments:
- features: bfloat16 [2048, 32768], P('rows', 'cols'), may hold values from -6 to 6
- block_rows: int32 [2, 512, 8], P(None, 'cols'), may hold values from 0 to 511, as said below
- weights: bfloat16 [2, 256, 512, 128], P(None, 'cols', 'rows'), may hold values from -0.375 to 0.375
- biases: float32 [2, 32768], P(None, 'cols'), may hold values from -0.5 to 0.2
Outputs:
- activations: bfloat16 [2048, 32768], P('rows', 'cols')
The draws below stay inside these ranges and needn't reach their ends.
Inputs may be any that keep to these rules, and one draw needn't show every extreme that they name: `block_rows`: the 8 block rows of one block column are distinct.
All inputs are finite; a program needn't handle non-finite values.
Results may differ from the reference program's by a relative error of at most 0.0051.
Values may be sent and summed in bfloat16 or wider, within the bound.
A program may use at most 128 MiB of HBM per device.

```python
import jax
import jax.numpy as jnp
from jax import lax

N = 32768
BS = 64
LAYERS = 2
ROW_DEV = 32
NB = 512
K = 8
ROWS = 2048
N_ROWS = 64


def draw_block_rows(key, part):
    key = jax.random.fold_in(key, 7)
    column_keys = jax.random.split(key, LAYERS * NB)
    chosen = jax.vmap(lambda one_key: jax.random.permutation(one_key, NB)[:K])(column_keys)
    return chosen.reshape(LAYERS, NB, K).astype(jnp.int32)


def block_levels(rng, dims, cuts, smallest, largest):
    def one(dim, blocks):
        heights = jax.random.uniform(jax.random.fold_in(jax.random.fold_in(rng, 6), dim), (blocks,), jnp.float32, smallest / len(cuts), largest / len(cuts))
        return jnp.repeat(jnp.exp(heights), dims[dim] // blocks).reshape((-1,) + (1,) * (len(dims) - dim - 1))

    factor_of = one(*cuts[0])
    for cut in cuts[1:]:
        factor_of = factor_of * one(*cut)
    return factor_of


def scatter_about(key, extent, deviation, most, cuts=(), kind=jnp.bfloat16):
    entries = deviation * jax.random.normal(key, extent, jnp.float32)
    if cuts:
        entries = entries * block_levels(key, extent, cuts, -0.22, 0.18)
    return jnp.clip(entries, -most, most).astype(kind)


def setup_inputs(seed: int = 0) -> dict:
    streams_of = jax.random.split(jax.random.key(seed), 5)
    features = scatter_about(streams_of[0], (ROWS, N), 1.0, 6.0, ((0, 64), (1, 4)))
    block_rows = draw_block_rows(jax.random.fold_in(streams_of[4], 71), 0)
    weights = scatter_about(streams_of[2], (LAYERS, NB // 2, K * BS, 2 * BS), (K * BS // 2) ** -0.5, 0.375, ((1, 4), (2, 64)))
    biases = jnp.clip(-0.5 + 0.7 * jax.random.uniform(streams_of[3], (LAYERS, N), jnp.float32) ** block_levels(streams_of[3], (LAYERS, N), ((1, 4),), -0.2, 0.2), -0.5, 0.2)
    return dict(features=features, block_rows=block_rows, weights=weights, biases=biases)


def apply_layer(full_rows, rows_of, tiles, bias_row):
    row_count = full_rows.shape[0]
    pair_count = tiles.shape[0]
    tile_depth = rows_of.shape[1]
    tile_size = tiles.shape[2] // 2
    panels = full_rows.reshape(row_count, -1, tile_size)
    picked = jnp.take(panels, rows_of.reshape(-1), axis=1)
    picked = picked.reshape(row_count, pair_count, 2, tile_depth, tile_size).astype(jnp.float32)
    blocks = tiles.reshape(pair_count, tile_depth, tile_size, 2, tile_size).astype(jnp.float32)
    totals = jnp.einsum("rphki,pkihj->rphj", picked, blocks)
    totals = totals.reshape(row_count, pair_count * 2 * tile_size) + bias_row
    return jnp.maximum(totals, 0.0).astype(jnp.bfloat16)


def reference(features, block_rows, weights, biases):
    current = features
    for layer_index in range(LAYERS):
        row_blocks = current.reshape(N_ROWS, ROW_DEV, N)
        current = lax.map(lambda part_rows: apply_layer(part_rows, block_rows[layer_index], weights[layer_index], biases[layer_index]), row_blocks)
        current = current.reshape(ROWS, N)
    return current
```

```python
import functools

import jax
import jax.numpy as jnp
from jax import lax
from jax.experimental import pallas as pl
from jax.experimental.pallas import tpu as pltpu
from jax.sharding import PartitionSpec as P

MESH = pl.DeviceIdType.MESH
NX, NY, NZ = 4, 4, 8
CHIPS = NX * NZ
PAIRS = 64
MINE = PAIRS // 2
HALF_ROWS = 32
ROWS = 2 * HALF_ROWS
LANES = 128
DIRS = ("x+", "x-", "z+", "z-")
SLOTS = 6

CHUNKS = (
    (0, 0, 6, 10),
    (0, 16, 7, 9),
    (1, 0, 6, 10),
    (1, 16, 7, 9),
)


def pieces_of(chunk, slot, direction):
    _, first, n_a, n_b = chunk
    a_cut, b_cut = n_a // 2, n_b - n_b // 2
    plus = direction[1] == "+"
    sign = 1 if plus else -1
    a_all, b_all = (first, n_a), (first + n_a, n_b)
    a_part = (first, a_cut) if plus else (first + a_cut, n_a - a_cut)
    b_part = (first + n_a, b_cut) if plus else (first + n_a + b_cut, n_b - b_cut)
    found = []
    if direction[0] == "z":
        for start, offset in ((1, 0), (2, 1), (2, -1), (3, 2)):
            step = slot - start
            if 0 <= step <= 2:
                found.append((offset, -sign * step, *a_all))
            elif step == 3:
                found.append((offset, -sign * step, *a_part))
        step = slot - 1
        if step <= 2:
            found.append((0, -sign * step, *b_all))
        elif step == 3:
            found.append((0, -sign * step, *b_part))
    else:
        if slot == 1:
            found.append((0, 0, *a_all))
        elif slot == 2:
            found.append((-sign, 0, *a_part))
        around = {0: (0,), 1: (1, -1), 2: (2, -2), 3: (3, -3), 4: (4,)}
        for far in around.get(slot - 1, ()):
            found.append((0, far, *b_all))
        for far in around.get(slot - 2, ()):
            found.append((-sign, far, *b_part))
    merged = []
    for piece in found:
        for at, other in enumerate(merged):
            if other[:2] == piece[:2] and other[2] + other[3] == piece[2]:
                merged[at] = (*other[:3], other[3] + piece[3])
                break
        else:
            merged.append(piece)
    return merged


def tiles_of(chunk, slot, direction):
    return sum(piece[3] for piece in pieces_of(chunk, slot, direction))


def kernel(
    index_ref, feat_ref, w_ref, bias_ref, out_ref,
    x_buf, y_buf, g_buf, part_buf, away, result,
    flood_send, flood_recv, part_send, part_recv, x_send, x_recv, y_send, y_recv, out_send, out_recv, out_sem,
):
    row, y = lax.axis_index("rows"), lax.axis_index("cols")
    core = row % 2
    z = (row // 2) % NZ
    x = row // (2 * NZ)

    def device(direction):
        nx, ny, nz, nc = x, y, z, core
        if direction == "c":
            nc = 1 - core
        else:
            step = 1 if direction[1] == "+" else -1
            if direction[0] == "x":
                nx = (x + step + NX) % NX
            elif direction[0] == "y":
                ny = (y + step + NY) % NY
            else:
                nz = (z + step + NZ) % NZ
        return ((nx * NZ + nz) * 2 + nc, ny)

    barrier = pltpu.get_barrier_semaphore()
    neighbours = DIRS + ("y+", "y-", "c")
    for direction in neighbours:
        pl.semaphore_signal(barrier, inc=1, device_id=device(direction), device_id_type=MESH)

    my_rows = pl.ds(pl.multiple_of(core * HALF_ROWS, HALF_ROWS), HALF_ROWS)

    def stage(step, carry):
        for more in range(8):
            pair = step * 8 + more
            x_buf[y * PAIRS + pair, my_rows, :] = feat_ref[:, pl.ds(pl.multiple_of(pair * LANES, LANES), LANES)]
        return carry

    lax.fori_loop(0, PAIRS // 8, stage, 0)
    pl.semaphore_wait(barrier, len(neighbours))

    def part_copy(layer):
        theirs = pl.ds(pl.multiple_of((1 - core) * MINE * 8, MINE * 8), MINE * 8)
        return pltpu.make_async_remote_copy(
            w_ref.at[layer, theirs], part_buf.at[layer], part_send.at[layer], part_recv.at[layer],
            device_id=device("c"), device_id_type=MESH,
        )

    part_copies = [part_copy(layer) for layer in range(2)]
    part_copies[0].start()

    def x_copy(number, offset, half, halves, direction):
        source = (y + offset + NY) % NY
        where = x_buf.at[pl.ds(source * PAIRS + half * (PAIRS // 2), halves * (PAIRS // 2)), my_rows]
        return pltpu.make_async_remote_copy(
            where, where, x_send.at[number], x_recv.at[number], device_id=device(direction), device_id_type=MESH
        )

    x_copies = {
        "+0": x_copy(0, 0, 0, 1, "y+"),
        "-1": x_copy(1, 0, 1, 1, "y-"),
        "+1": x_copy(2, 0, 1, 1, "y+"),
        "-0": x_copy(3, 0, 0, 1, "y-"),
        "++0": x_copy(4, -1, 0, 1, "y+"),
        "--1": x_copy(5, 1, 1, 1, "y-"),
        "c": x_copy(6, 0, 0, 2, "c"),
        "c+0": x_copy(7, -1, 0, 1, "c"),
        "c-1": x_copy(8, 1, 1, 1, "c"),
        "c+1": x_copy(9, -1, 1, 1, "c"),
        "c-0": x_copy(10, 1, 0, 1, "c"),
        "c++0": x_copy(11, 2, 0, 1, "c"),
        "c--1": x_copy(12, 2, 1, 1, "c"),
    }
    for name in ("+0", "-1", "+1", "-0"):
        x_copies[name].start()
    part_copies[1].start()

    def merge(layer):
        part_copies[layer].wait_recv()
        ours = pl.ds(pl.multiple_of(core * MINE * 8, MINE * 8), MINE * 8)
        own = w_ref[layer, ours, :].astype(jnp.float32).reshape(MINE, 8, LANES)
        other = part_buf[layer].astype(jnp.float32).reshape(MINE, 8, LANES)
        first = core == 0
        both = jnp.concatenate([jnp.where(first, own, other), jnp.where(first, other, own)], axis=1)
        base = ((layer * NX + x) * NZ + z) * MINE
        g_buf[pl.ds(base, MINE)] = both.astype(jnp.bfloat16)

    def flood_copy(number, slot, direction, piece):
        dx, dz, first, count = piece
        layer = CHUNKS[number][0]
        base = ((layer * NX + (x + dx + NX) % NX) * NZ + (z + dz + NZ) % NZ) * MINE + first
        where = g_buf.at[pl.ds(base, count)]
        at = DIRS.index(direction)
        return pltpu.make_async_remote_copy(
            where, where, flood_send.at[number, at], flood_recv.at[number, slot - 1, at],
            device_id=device(direction), device_id_type=MESH,
        )

    def flood_issue(number, slot):
        for direction in DIRS:
            for piece in pieces_of(CHUNKS[number], slot, direction):
                flood_copy(number, slot, direction, piece).start()

    def flood_arrived(number, slot):
        for direction in DIRS:
            total = tiles_of(CHUNKS[number], slot, direction)
            at = DIRS.index(direction)
            where = g_buf.at[pl.ds(0, total)]
            pltpu.make_async_remote_copy(
                where, where, flood_send.at[number, at], flood_recv.at[number, slot - 1, at],
                device_id=device(direction), device_id_type=MESH,
            ).wait_recv()

    def flood_sent(number):
        for direction in DIRS:
            total = sum(tiles_of(CHUNKS[number], slot, direction) for slot in range(1, SLOTS + 1))
            at = DIRS.index(direction)
            where = g_buf.at[pl.ds(0, total)]
            pltpu.make_async_remote_copy(
                where, where, flood_send.at[number, at], flood_recv.at[number, 0, at],
                device_id=device(direction), device_id_type=MESH,
            ).wait_send()

    def flood_step(number, slot):
        flood_arrived(number, slot - 1)
        if slot <= SLOTS:
            flood_issue(number, slot)

    lane = lax.broadcasted_iota(jnp.int32, (ROWS, LANES), 1)
    low = lane < LANES // 2

    def pair_tile(layer, pair, panels):
        sides = []
        for h in range(2):
            at = layer * PAIRS * 16 + (core * MINE + pair) * 16 + h * 8
            tiles = []
            for k in range(0, 8, 2):
                one, two = index_ref[at + k], index_ref[at + k + 1]
                a, b = panels[one // 2], panels[two // 2]
                a = jnp.where(one % 2 == 1, pltpu.roll(a, LANES // 2, 1), a)
                b = jnp.where(two % 2 == 0, pltpu.roll(b, LANES // 2, 1), b)
                tiles.append(jnp.where(low, a, b))
            sides.append(jnp.concatenate(tiles, axis=1))
        picked = jnp.concatenate(sides, axis=0)
        w = jnp.concatenate([g_buf[(layer * CHIPS + chip) * MINE + pair] for chip in range(CHIPS)], axis=0)
        total = jnp.dot(picked, w, preferred_element_type=jnp.float32)
        total = jnp.where(low, total[:ROWS], total[ROWS:])
        total = total + bias_ref[layer, pl.ds(core * MINE + pair, 1), :]
        return jnp.maximum(total, 0.0).astype(jnp.bfloat16)

    quarter = MINE // 4

    def y_copy(number, offset, part, direction):
        source = (y + offset + NY) % NY
        where = y_buf.at[pl.ds(source * PAIRS + core * MINE + part * quarter, quarter)]
        return pltpu.make_async_remote_copy(
            where, where, y_send.at[number], y_recv.at[number], device_id=device(direction), device_id_type=MESH
        )

    y_copies = {}
    for part in range(4):
        y_copies["+", part] = y_copy(part, 0, part, "y+")
        y_copies["-", part] = y_copy(4 + part, 0, part, "y-")
        y_copies["c", part] = y_copy(8 + part, 0, part, "c")
        y_copies["c+", part] = y_copy(12 + part, -1, part, "c")
        y_copies["c-", part] = y_copy(16 + part, 1, part, "c")
        y_copies["cc", part] = y_copy(20 + part, 2, part, "c")
        if part < 2:
            y_copies["++", part] = y_copy(24 + part, -1, part, "y+")
        else:
            y_copies["--", part] = y_copy(24 + part, 1, part, "y-")

    def layer_one(part):
        def step(at, carry):
            pair = part * quarter + at
            y_buf[y * PAIRS + core * MINE + pair] = pair_tile(0, pair, x_buf)
            return carry

        lax.fori_loop(0, quarter, step, 0)

    def layer_two(part):
        def step(at, carry):
            pair = part * quarter + at
            tile = pair_tile(1, pair, y_buf)
            first = core == 0
            ours = jnp.where(first, tile[:HALF_ROWS], tile[HALF_ROWS:])
            theirs = jnp.where(first, tile[HALF_ROWS:], tile[:HALF_ROWS])
            result[:, pl.ds(pl.multiple_of((core * MINE + pair) * LANES, LANES), LANES)] = ours
            away[:, pl.ds(pl.multiple_of(pair * LANES, LANES), LANES)] = theirs
            return carry

        lax.fori_loop(0, quarter, step, 0)

    def out_copy(part):
        width = quarter * LANES
        there = pl.ds(pl.multiple_of((core * MINE + part * quarter) * LANES, width), width)
        return pltpu.make_async_remote_copy(
            away.at[:, pl.ds(part * width, width)], result.at[:, there], out_send.at[part], out_recv.at[part],
            device_id=device("c"), device_id_type=MESH,
        )

    merge(0)
    flood_issue(0, 1)
    flood_issue(1, 1)
    x_copies["c"].start()
    merge(1)
    flood_step(0, 2)
    flood_step(1, 2)
    x_copies["+0"].wait_recv()
    x_copies["++0"].start()
    x_copies["c+0"].start()
    x_copies["-1"].wait_recv()
    x_copies["--1"].start()
    x_copies["c-1"].start()
    flood_step(0, 3)
    flood_step(1, 3)
    flood_step(0, 4)
    x_copies["+1"].wait_recv()
    x_copies["c+1"].start()
    x_copies["-0"].wait_recv()
    x_copies["c-0"].start()
    flood_step(1, 4)
    flood_issue(2, 1)
    flood_step(0, 5)
    flood_issue(3, 1)
    flood_step(1, 5)
    flood_step(2, 2)
    flood_step(0, 6)
    x_copies["++0"].wait_recv()
    x_copies["c++0"].start()
    x_copies["--1"].wait_recv()
    x_copies["c--1"].start()
    flood_step(1, 6)
    flood_step(3, 2)
    flood_step(2, 3)
    for name in ("c", "c+0", "c-1", "c+1", "c-0", "c++0", "c--1"):
        x_copies[name].wait_recv()
    flood_step(0, 7)
    layer_one(0)
    for name in ("+", "-", "c"):
        y_copies[name, 0].start()
    flood_step(3, 3)
    layer_one(1)
    for name in ("+", "c"):
        y_copies[name, 1].start()
    flood_step(1, 7)
    layer_one(2)
    for name in ("-", "+", "c"):
        y_copies[name, 2].start()
    flood_step(2, 4)
    layer_one(3)
    for name in ("-", "+", "c"):
        y_copies[name, 3].start()
    y_copies["-", 1].start()
    flood_step(3, 4)

    def passed(way, part, on):
        y_copies[way, part].wait_recv()
        if on:
            y_copies[way * 2, part].start()
        y_copies["c" + way, part].start()

    passed("+", 0, True)
    passed("-", 0, False)
    passed("+", 1, True)
    flood_step(2, 5)
    passed("-", 2, True)
    flood_step(3, 5)
    passed("+", 2, False)
    passed("-", 3, True)
    passed("+", 3, False)
    passed("-", 1, False)
    flood_step(2, 6)
    flood_step(3, 6)
    for way, part in (("++", 0), ("--", 2), ("++", 1), ("--", 3)):
        y_copies[way, part].wait_recv()
        y_copies["cc", part].start()
    flood_step(2, 7)
    flood_step(3, 7)
    for way in ("c", "c+", "c-", "cc"):
        for part in range(4):
            y_copies[way, part].wait_recv()
    out_copies = [out_copy(part) for part in range(4)]
    for part in range(4):
        layer_two(part)
        out_copies[part].start()

    for copy in part_copies + list(x_copies.values()) + list(y_copies.values()):
        copy.wait_send()
    for number in range(len(CHUNKS)):
        flood_sent(number)
    for copy in out_copies:
        copy.wait()
    done = pltpu.make_async_copy(result, out_ref, out_sem)
    done.start()
    done.wait()


def shards(features, block_rows, weights, biases):
    vmem = pl.BlockSpec(memory_space=pltpu.VMEM)
    return pl.pallas_call(
        kernel,
        out_shape=jax.ShapeDtypeStruct((HALF_ROWS, PAIRS * LANES), jnp.bfloat16),
        in_specs=[pl.BlockSpec(memory_space=pltpu.SMEM), vmem, vmem, vmem],
        out_specs=pl.BlockSpec(memory_space=pl.ANY),
        scratch_shapes=[
            pltpu.VMEM((NY * PAIRS, ROWS, LANES), jnp.bfloat16),
            pltpu.VMEM((NY * PAIRS, ROWS, LANES), jnp.bfloat16),
            pltpu.VMEM((2 * CHIPS * MINE, 16, LANES), jnp.bfloat16),
            pltpu.VMEM((2, MINE * 8, LANES), jnp.bfloat16),
            pltpu.VMEM((HALF_ROWS, MINE * LANES), jnp.bfloat16),
            pltpu.VMEM((HALF_ROWS, PAIRS * LANES), jnp.bfloat16),
            pltpu.SemaphoreType.DMA((len(CHUNKS), 4)),
            pltpu.SemaphoreType.DMA((len(CHUNKS), SLOTS, 4)),
            pltpu.SemaphoreType.DMA((2,)),
            pltpu.SemaphoreType.DMA((2,)),
            pltpu.SemaphoreType.DMA((13,)),
            pltpu.SemaphoreType.DMA((13,)),
            pltpu.SemaphoreType.DMA((28,)),
            pltpu.SemaphoreType.DMA((28,)),
            pltpu.SemaphoreType.DMA((4,)),
            pltpu.SemaphoreType.DMA((4,)),
            pltpu.SemaphoreType.DMA,
        ],
        compiler_params=pltpu.CompilerParams(
            collective_id=0, has_side_effects=True, vmem_limit_bytes=40 << 20
        ),
    )(
        block_rows.reshape(-1),
        features,
        weights.reshape(2, PAIRS * 8, LANES),
        biases.reshape(2, PAIRS, LANES),
    )


def solution(mesh):
    return jax.shard_map(
        shards,
        mesh=mesh,
        in_specs=(
            P("rows", "cols"),
            P(None, "cols", None),
            P(None, "cols", "rows", None),
            P(None, "cols"),
        ),
        out_specs=P("rows", "cols"),
        check_vma=False,
    )
```

```python
import functools

import jax
import jax.numpy as jnp
from jax import lax
from jax.experimental import pallas as pl
from jax.experimental.pallas import tpu as pltpu
from jax.sharding import PartitionSpec as P

MESH = pl.DeviceIdType.MESH
NX, NY, NZ = 4, 4, 8
CHIPS = NX * NZ
PAIRS = 64
MINE = PAIRS // 2
HALF_ROWS = 32
ROWS = 2 * HALF_ROWS
LANES = 128
DIRS = ("x+", "x-", "z+", "z-")
SLOTS = 6

CHUNKS = (
    (0, 0, 3, 5),
    (0, 8, 4, 4),
    (0, 16, 3, 5),
    (0, 24, 3, 5),
    (1, 0, 3, 5),
    (1, 8, 4, 4),
    (1, 16, 3, 5),
    (1, 24, 3, 5),
)
PARTS = 4
ORDER = (
    ("own",), ("merge", 0), ("flood", 0, 1), ("merge", 1), ("flood", 1, 1), ("flood", 2, 1), ("flood", 3, 1),
    ("flood", 4, 1), ("flood", 0, 2), ("flood", 1, 2), ("flood", 2, 2), ("x", "+0"), ("x", "-1"), ("flood", 3, 2),
    ("flood", 0, 3), ("flood", 1, 3), ("flood", 2, 3), ("flood", 3, 3), ("x", "+1"), ("x", "-0"), ("flood", 0, 4),
    ("flood", 4, 2), ("flood", 1, 4), ("flood", 2, 4), ("flood", 3, 4), ("x", "++0"), ("x", "--1"), ("flood", 0, 5),
    ("flood", 4, 3), ("x_all",), ("flood", 5, 1), ("flood", 1, 5), ("flood", 2, 5), ("flood", 7, 1), ("flood", 3, 5),
    ("flood", 0, 6), ("flood", 6, 1), ("flood", 4, 4), ("flood", 1, 6), ("flood", 5, 2), ("flood", 2, 6),
    ("flood", 7, 2), ("flood", 0, 7), ("one", 0), ("flood", 3, 6), ("flood", 6, 2), ("flood", 1, 7), ("one", 1),
    ("flood", 4, 5), ("flood", 2, 7), ("one", 2), ("flood", 3, 7), ("one", 3), ("flood", 5, 3), ("y", "+", 0),
    ("y", "-", 0), ("flood", 4, 6), ("flood", 7, 3), ("flood", 6, 3), ("y", "+", 1), ("y", "-", 1), ("flood", 5, 4),
    ("flood", 4, 7), ("y", "+", 2), ("y", "-", 2), ("flood", 7, 4), ("flood", 6, 4), ("y", "+", 3), ("y", "-", 3),
    ("flood", 5, 5), ("flood", 7, 5), ("y", "++", 0), ("y", "--", 2), ("flood", 6, 5), ("flood", 5, 6),
    ("flood", 7, 6), ("y", "++", 1), ("y", "--", 3), ("flood", 6, 6), ("flood", 5, 7), ("y_all",), ("two", 0),
    ("flood", 7, 7), ("two", 1), ("flood", 6, 7), ("two", 2), ("two", 3),
)


def pieces_of(chunk, slot, direction):
    _, first, n_a, n_b = chunk
    a_cut, b_cut = n_a // 2, n_b - n_b // 2
    plus = direction[1] == "+"
    sign = 1 if plus else -1
    a_all, b_all = (first, n_a), (first + n_a, n_b)
    a_part = (first, a_cut) if plus else (first + a_cut, n_a - a_cut)
    b_part = (first + n_a, b_cut) if plus else (first + n_a + b_cut, n_b - b_cut)
    found = []
    if direction[0] == "z":
        for start, offset in ((1, 0), (2, 1), (2, -1), (3, 2)):
            step = slot - start
            if 0 <= step <= 2:
                found.append((offset, -sign * step, *a_all))
            elif step == 3:
                found.append((offset, -sign * step, *a_part))
        step = slot - 1
        if step <= 2:
            found.append((0, -sign * step, *b_all))
        elif step == 3:
            found.append((0, -sign * step, *b_part))
    else:
        if slot == 1:
            found.append((0, 0, *a_all))
        elif slot == 2:
            found.append((-sign, 0, *a_part))
        around = {0: (0,), 1: (1, -1), 2: (2, -2), 3: (3, -3), 4: (4,)}
        for far in around.get(slot - 1, ()):
            found.append((0, far, *b_all))
        for far in around.get(slot - 2, ()):
            found.append((-sign, far, *b_part))
    merged = []
    for piece in found:
        for at, other in enumerate(merged):
            if other[:2] == piece[:2] and other[2] + other[3] == piece[2]:
                merged[at] = (*other[:3], other[3] + piece[3])
                break
        else:
            merged.append(piece)
    return merged


def tiles_of(chunk, slot, direction):
    return sum(piece[3] for piece in pieces_of(chunk, slot, direction))


def kernel(
    index_ref, feat_ref, w_ref, bias_ref, out_ref,
    x_buf, y_buf, g_buf, w_buf, part_buf, away,
    flood_send, flood_recv, part_send, part_recv, x_send, x_recv, y_send, y_recv, out_send, out_recv, x_in, w_in,
):
    row, y = lax.axis_index("rows"), lax.axis_index("cols")
    core = row % 2
    z = (row // 2) % NZ
    x = row // (2 * NZ)

    def device(direction):
        nx, ny, nz, nc = x, y, z, core
        if direction == "c":
            nc = 1 - core
        else:
            step = 1 if direction[1] == "+" else -1
            if direction[0] == "x":
                nx = (x + step + NX) % NX
            elif direction[0] == "y":
                ny = (y + step + NY) % NY
            else:
                nz = (z + step + NZ) % NZ
        return ((nx * NZ + nz) * 2 + nc, ny)

    barrier = pltpu.get_barrier_semaphore()
    neighbours = DIRS + ("y+", "y-", "c")
    for direction in neighbours:
        pl.semaphore_signal(barrier, inc=1, device_id=device(direction), device_id_type=MESH)

    my_rows = pl.ds(pl.multiple_of(core * HALF_ROWS, HALF_ROWS), HALF_ROWS)
    w_copy = pltpu.make_async_copy(w_ref, w_buf, w_in)
    w_copy.start()

    def stage(step, carry):
        for more in range(8):
            pair = step * 8 + more
            columns = pl.ds(pl.multiple_of(pair * LANES, LANES), LANES)
            pltpu.make_async_copy(feat_ref.at[:, columns], x_buf.at[y * PAIRS + pair, my_rows], x_in).start()
        return carry

    lax.fori_loop(0, PAIRS // 8, stage, 0)
    w_copy.wait()
    pl.semaphore_wait(barrier, len(neighbours))

    def part_copy(layer):
        theirs = pl.ds(pl.multiple_of((1 - core) * MINE * 8, MINE * 8), MINE * 8)
        return pltpu.make_async_remote_copy(
            w_buf.at[layer, theirs], part_buf.at[layer], part_send.at[layer], part_recv.at[layer],
            device_id=device("c"), device_id_type=MESH,
        )

    part_copies = [part_copy(layer) for layer in range(2)]
    part_copies[0].start()

    def x_copy(number, offset, half, halves, direction):
        source = (y + offset + NY) % NY
        where = x_buf.at[pl.ds(source * PAIRS + half * (PAIRS // 2), halves * (PAIRS // 2)), my_rows]
        return pltpu.make_async_remote_copy(
            where, where, x_send.at[number], x_recv.at[number], device_id=device(direction), device_id_type=MESH
        )

    x_copies = {
        "+0": x_copy(0, 0, 0, 1, "y+"),
        "-1": x_copy(1, 0, 1, 1, "y-"),
        "+1": x_copy(2, 0, 1, 1, "y+"),
        "-0": x_copy(3, 0, 0, 1, "y-"),
        "++0": x_copy(4, -1, 0, 1, "y+"),
        "--1": x_copy(5, 1, 1, 1, "y-"),
        "c": x_copy(6, 0, 0, 2, "c"),
        "c+0": x_copy(7, -1, 0, 1, "c"),
        "c-1": x_copy(8, 1, 1, 1, "c"),
        "c+1": x_copy(9, -1, 1, 1, "c"),
        "c-0": x_copy(10, 1, 0, 1, "c"),
        "c++0": x_copy(11, 2, 0, 1, "c"),
        "c--1": x_copy(12, 2, 1, 1, "c"),
    }
    part_copies[1].start()
    mine = x_buf.at[pl.ds(y * PAIRS, PAIRS), my_rows]
    pltpu.make_async_copy(mine, mine, x_in).wait()

    def merge(layer):
        part_copies[layer].wait_recv()
        ours = pl.ds(pl.multiple_of(core * MINE * 8, MINE * 8), MINE * 8)
        own = w_buf[layer, ours, :].astype(jnp.float32).reshape(MINE, 8, LANES)
        other = part_buf[layer].astype(jnp.float32).reshape(MINE, 8, LANES)
        first = core == 0
        both = jnp.concatenate([jnp.where(first, own, other), jnp.where(first, other, own)], axis=1)
        base = ((layer * NX + x) * NZ + z) * MINE
        g_buf[pl.ds(base, MINE)] = both.astype(jnp.bfloat16)

    def flood_copy(number, slot, direction, piece):
        dx, dz, first, count = piece
        layer = CHUNKS[number][0]
        base = ((layer * NX + (x + dx + NX) % NX) * NZ + (z + dz + NZ) % NZ) * MINE + first
        where = g_buf.at[pl.ds(base, count)]
        at = DIRS.index(direction)
        return pltpu.make_async_remote_copy(
            where, where, flood_send.at[number, at], flood_recv.at[number, slot - 1, at],
            device_id=device(direction), device_id_type=MESH,
        )

    def flood_issue(number, slot):
        for direction in DIRS:
            for piece in pieces_of(CHUNKS[number], slot, direction):
                flood_copy(number, slot, direction, piece).start()

    def flood_arrived(number, slot):
        for direction in DIRS:
            total = tiles_of(CHUNKS[number], slot, direction)
            at = DIRS.index(direction)
            where = g_buf.at[pl.ds(0, total)]
            pltpu.make_async_remote_copy(
                where, where, flood_send.at[number, at], flood_recv.at[number, slot - 1, at],
                device_id=device(direction), device_id_type=MESH,
            ).wait_recv()

    def flood_sent(number):
        for direction in DIRS:
            total = sum(tiles_of(CHUNKS[number], slot, direction) for slot in range(1, SLOTS + 1))
            at = DIRS.index(direction)
            where = g_buf.at[pl.ds(0, total)]
            pltpu.make_async_remote_copy(
                where, where, flood_send.at[number, at], flood_recv.at[number, 0, at],
                device_id=device(direction), device_id_type=MESH,
            ).wait_send()

    def flood_step(number, slot):
        flood_arrived(number, slot - 1)
        if slot <= SLOTS:
            flood_issue(number, slot)

    lane = lax.broadcasted_iota(jnp.int32, (ROWS, LANES), 1)
    low = lane < LANES // 2

    def pair_tile(layer, pair, panels):
        sides = []
        for h in range(2):
            column = (core * MINE + pair) * 2 + h
            tiles = []
            for k in range(0, 8, 2):
                one, two = index_ref[layer, k, column], index_ref[layer, k + 1, column]
                a, b = panels[one // 2], panels[two // 2]
                a = jnp.where(one % 2 == 1, pltpu.roll(a, LANES // 2, 1), a)
                b = jnp.where(two % 2 == 0, pltpu.roll(b, LANES // 2, 1), b)
                tiles.append(jnp.where(low, a, b))
            sides.append(jnp.concatenate(tiles, axis=1))
        picked = jnp.concatenate(sides, axis=0)
        w = jnp.concatenate([g_buf[(layer * CHIPS + chip) * MINE + pair] for chip in range(CHIPS)], axis=0)
        total = jnp.dot(picked, w, preferred_element_type=jnp.float32)
        total = jnp.where(low, total[:ROWS], total[ROWS:])
        total = total + bias_ref[layer : layer + 1, pl.ds(pl.multiple_of((core * MINE + pair) * LANES, LANES), LANES)]
        return jnp.maximum(total, 0.0).astype(jnp.bfloat16)

    share = MINE // PARTS

    def y_copy(number, offset, part, direction):
        source = (y + offset + NY) % NY
        where = y_buf.at[pl.ds(source * PAIRS + core * MINE + part * share, share)]
        return pltpu.make_async_remote_copy(
            where, where, y_send.at[number], y_recv.at[number], device_id=device(direction), device_id_type=MESH
        )

    y_copies = {}
    for part in range(PARTS):
        y_copies["+", part] = y_copy(part, 0, part, "y+")
        y_copies["-", part] = y_copy(PARTS + part, 0, part, "y-")
        y_copies["c", part] = y_copy(2 * PARTS + part, 0, part, "c")
        y_copies["c+", part] = y_copy(3 * PARTS + part, -1, part, "c")
        y_copies["c-", part] = y_copy(4 * PARTS + part, 1, part, "c")
        y_copies["cc", part] = y_copy(5 * PARTS + part, 2, part, "c")
        if part < PARTS // 2:
            y_copies["++", part] = y_copy(6 * PARTS + part, -1, part, "y+")
        else:
            y_copies["--", part] = y_copy(6 * PARTS + part, 1, part, "y-")

    def layer_one(part):
        def step(at, carry):
            pair = part * share + at
            y_buf[y * PAIRS + core * MINE + pair] = pair_tile(0, pair, x_buf)
            return carry

        lax.fori_loop(0, share, step, 0, unroll=share)

    def layer_two(part):
        def step(at, carry):
            pair = part * share + at
            tile = pair_tile(1, pair, y_buf)
            first = core == 0
            ours = jnp.where(first, tile[:HALF_ROWS], tile[HALF_ROWS:])
            theirs = jnp.where(first, tile[HALF_ROWS:], tile[:HALF_ROWS])
            out_ref[:, pl.ds(pl.multiple_of((core * MINE + pair) * LANES, LANES), LANES)] = ours
            away[:, pl.ds(pl.multiple_of(pair * LANES, LANES), LANES)] = theirs
            return carry

        lax.fori_loop(0, share, step, 0, unroll=share)

    def out_copy(part):
        width = share * LANES
        there = pl.ds(pl.multiple_of((core * MINE + part * share) * LANES, width), width)
        return pltpu.make_async_remote_copy(
            away.at[:, pl.ds(part * width, width)], out_ref.at[:, there], out_send.at[part], out_recv.at[part],
            device_id=device("c"), device_id_type=MESH,
        )

    out_copies = [out_copy(part) for part in range(PARTS)]

    def x_step(name):
        x_copies[name].wait_recv()
        if name == "+0":
            x_copies["++0"].start()
        if name == "-1":
            x_copies["--1"].start()
        x_copies["c" + name].start()

    def y_step(way, part):
        y_copies[way, part].wait_recv()
        if (way, part < PARTS // 2) in (("+", True), ("-", False)):
            y_copies[way * 2, part].start()
        y_copies["cc" if len(way) == 2 else "c" + way, part].start()

    for task in ORDER:
        kind, *rest = task
        if kind == "own":
            for name in ("+0", "-1", "+1", "-0", "c"):
                x_copies[name].start()
        elif kind == "merge":
            merge(*rest)
        elif kind == "flood":
            number, slot = rest
            if slot > 1:
                flood_arrived(number, slot - 1)
            if slot <= SLOTS:
                flood_issue(number, slot)
        elif kind == "x":
            x_step(*rest)
        elif kind == "x_all":
            for name in ("c", "c+0", "c-1", "c+1", "c-0", "c++0", "c--1"):
                x_copies[name].wait_recv()
        elif kind == "one":
            (part,) = rest
            layer_one(part)
            for way in ("+", "-", "c"):
                y_copies[way, part].start()
        elif kind == "y":
            y_step(*rest)
        elif kind == "y_all":
            for way in ("c", "c+", "c-", "cc"):
                for part in range(PARTS):
                    y_copies[way, part].wait_recv()
        else:
            (part,) = rest
            layer_two(part)
            out_copies[part].start()

    for copy in part_copies + list(x_copies.values()) + list(y_copies.values()):
        copy.wait_send()
    for number in range(len(CHUNKS)):
        flood_sent(number)
    for copy in out_copies:
        copy.wait()


def shards(features, block_rows, weights, biases):
    vmem = pl.BlockSpec(memory_space=pltpu.VMEM)
    anywhere = pl.BlockSpec(memory_space=pl.ANY)
    return pl.pallas_call(
        kernel,
        out_shape=jax.ShapeDtypeStruct((HALF_ROWS, PAIRS * LANES), jnp.bfloat16),
        in_specs=[pl.BlockSpec(memory_space=pltpu.SMEM), anywhere, anywhere, vmem],
        out_specs=vmem,
        scratch_shapes=[
            pltpu.VMEM((NY * PAIRS, ROWS, LANES), jnp.bfloat16),
            pltpu.VMEM((NY * PAIRS, ROWS, LANES), jnp.bfloat16),
            pltpu.VMEM((2 * CHIPS * MINE, 16, LANES), jnp.bfloat16),
            pltpu.VMEM((2, PAIRS * 8, LANES), jnp.bfloat16),
            pltpu.VMEM((2, MINE * 8, LANES), jnp.bfloat16),
            pltpu.VMEM((HALF_ROWS, MINE * LANES), jnp.bfloat16),
            pltpu.SemaphoreType.DMA((len(CHUNKS), 4)),
            pltpu.SemaphoreType.DMA((len(CHUNKS), SLOTS, 4)),
            pltpu.SemaphoreType.DMA((2,)),
            pltpu.SemaphoreType.DMA((2,)),
            pltpu.SemaphoreType.DMA((13,)),
            pltpu.SemaphoreType.DMA((13,)),
            pltpu.SemaphoreType.DMA((7 * PARTS,)),
            pltpu.SemaphoreType.DMA((7 * PARTS,)),
            pltpu.SemaphoreType.DMA((PARTS,)),
            pltpu.SemaphoreType.DMA((PARTS,)),
            pltpu.SemaphoreType.DMA,
            pltpu.SemaphoreType.DMA,
        ],
        compiler_params=pltpu.CompilerParams(
            collective_id=0, has_side_effects=True, vmem_limit_bytes=56 << 20
        ),
    )(
        block_rows.transpose(0, 2, 1),
        features,
        weights.reshape(2, PAIRS * 8, LANES),
        biases,
    )


def solution(mesh):
    return jax.shard_map(
        shards,
        mesh=mesh,
        in_specs=(
            P("rows", "cols"),
            P(None, "cols", None),
            P(None, "cols", "rows", None),
            P(None, "cols"),
        ),
        out_specs=P("rows", "cols"),
        check_vma=False,
    )
```

```python
import functools

import jax
import jax.numpy as jnp
from jax import lax
from jax.experimental import pallas as pl
from jax.experimental.pallas import tpu as pltpu
from jax.sharding import PartitionSpec as P

MESH = pl.DeviceIdType.MESH
NX, NY, NZ = 4, 4, 8
CHIPS = NX * NZ
PAIRS = 64
MINE = PAIRS // 2
HALF_ROWS = 32
ROWS = 2 * HALF_ROWS
LANES = 128
DIRS = ("x+", "x-", "z+", "z-")
SLOTS = 6

CHUNKS = (
    (0, 0, 2, 2),
    (0, 4, 1, 3),
    (0, 8, 4, 4),
    (0, 16, 3, 5),
    (0, 24, 3, 5),
    (1, 0, 3, 5),
    (1, 8, 4, 4),
    (1, 16, 3, 5),
    (1, 24, 3, 5),
)
PARTS = 4
ORDER = (
    ("merge", 0), ("flood", 2, 1), ("merge", 1), ("flood", 0, 1), ("flood", 1, 1), ("flood", 3, 1), ("own",),
    ("flood", 6, 1), ("flood", 4, 1), ("flood", 5, 1), ("flood", 2, 2), ("flood", 0, 2), ("flood", 1, 2),
    ("flood", 3, 2), ("flood", 7, 1), ("flood", 2, 3), ("flood", 1, 3), ("flood", 0, 3), ("flood", 4, 2),
    ("flood", 3, 3), ("x", "+0"), ("x", "-1"), ("flood", 2, 4), ("flood", 1, 4), ("flood", 0, 4), ("flood", 4, 3),
    ("flood", 3, 4), ("x", "+1"), ("flood", 2, 5), ("flood", 1, 5), ("flood", 0, 5), ("x", "--1"), ("x", "-0"),
    ("flood", 5, 2), ("x", "++0"), ("flood", 7, 2), ("flood", 3, 5), ("flood", 2, 6), ("x_all",), ("flood", 0, 6),
    ("roll", 0), ("flood", 1, 6), ("flood", 8, 1), ("flood", 4, 4), ("flood", 5, 3), ("roll", 1), ("roll", 3),
    ("roll", 2), ("flood", 3, 6), ("flood", 2, 7), ("flood", 6, 2), ("flood", 0, 7), ("flood", 1, 7), ("one", 0),
    ("flood", 4, 5), ("flood", 7, 3), ("one", 1), ("flood", 8, 2), ("flood", 4, 6), ("flood", 3, 7), ("flood", 6, 3),
    ("one", 2), ("flood", 7, 4), ("flood", 8, 3), ("flood", 4, 7), ("one", 3), ("y", "-", 1), ("flood", 5, 4),
    ("y", "+", 0), ("y_in", 0), ("flood", 6, 4), ("y", "+", 1), ("flood", 7, 5), ("y", "-", 2), ("flood", 8, 4),
    ("flood", 5, 5), ("y", "-", 3), ("y", "+", 3), ("flood", 6, 5), ("flood", 8, 5), ("flood", 7, 6), ("y", "+", 2),
    ("flood", 5, 6), ("flood", 6, 6), ("y", "++", 0), ("y", "--", 2), ("y", "-", 0), ("y", "--", 3), ("y_in", 1),
    ("y", "++", 1), ("y_in", 2), ("flood", 7, 7), ("flood", 8, 6), ("y_in", 3), ("flood", 6, 7), ("flood", 5, 7),
    ("two", 0), ("two", 1), ("two", 2), ("flood", 8, 7), ("two", 3),
)


def pieces_of(chunk, slot, direction):
    _, first, n_a, n_b = chunk
    a_cut, b_cut = n_a // 2, n_b - n_b // 2
    plus = direction[1] == "+"
    sign = 1 if plus else -1
    a_all, b_all = (first, n_a), (first + n_a, n_b)
    a_part = (first, a_cut) if plus else (first + a_cut, n_a - a_cut)
    b_part = (first + n_a, b_cut) if plus else (first + n_a + b_cut, n_b - b_cut)
    found = []
    if direction[0] == "z":
        for start, offset in ((1, 0), (2, 1), (2, -1), (3, 2)):
            step = slot - start
            if 0 <= step <= 2:
                found.append((offset, -sign * step, *a_all))
            elif step == 3:
                found.append((offset, -sign * step, *a_part))
        step = slot - 1
        if step <= 2:
            found.append((0, -sign * step, *b_all))
        elif step == 3:
            found.append((0, -sign * step, *b_part))
    else:
        if slot == 1:
            found.append((0, 0, *a_all))
        elif slot == 2:
            found.append((-sign, 0, *a_part))
        around = {0: (0,), 1: (1, -1), 2: (2, -2), 3: (3, -3), 4: (4,)}
        for far in around.get(slot - 1, ()):
            found.append((0, far, *b_all))
        for far in around.get(slot - 2, ()):
            found.append((-sign, far, *b_part))
    merged = []
    for piece in found:
        if piece[3] == 0:
            continue
        for at, other in enumerate(merged):
            if other[:2] == piece[:2] and other[2] + other[3] == piece[2]:
                merged[at] = (*other[:3], other[3] + piece[3])
                break
        else:
            merged.append(piece)
    return merged


def tiles_of(chunk, slot, direction):
    return sum(piece[3] for piece in pieces_of(chunk, slot, direction))


def kernel(
    index_ref, feat_ref, w_ref, bias_ref, out_ref,
    x_buf, y_buf, g_buf, w_buf, part_buf, away,
    flood_send, flood_recv, part_send, part_recv, x_send, x_recv, y_send, y_recv, out_send, out_recv, x_in, w_in,
):
    row, y = lax.axis_index("rows"), lax.axis_index("cols")
    core = row % 2
    z = (row // 2) % NZ
    x = row // (2 * NZ)

    def device(direction):
        nx, ny, nz, nc = x, y, z, core
        if direction == "c":
            nc = 1 - core
        else:
            step = 1 if direction[1] == "+" else -1
            if direction[0] == "x":
                nx = (x + step + NX) % NX
            elif direction[0] == "y":
                ny = (y + step + NY) % NY
            else:
                nz = (z + step + NZ) % NZ
        return ((nx * NZ + nz) * 2 + nc, ny)

    barrier = pltpu.get_barrier_semaphore()
    neighbours = DIRS + ("y+", "y-", "c")
    for direction in neighbours:
        pl.semaphore_signal(barrier, inc=1, device_id=device(direction), device_id_type=MESH)

    my_rows = pl.ds(pl.multiple_of(core * HALF_ROWS, HALF_ROWS), HALF_ROWS)
    w_copy = pltpu.make_async_copy(w_ref, w_buf, w_in)
    w_copy.start()

    def stage(step, carry):
        for more in range(8):
            pair = step * 8 + more
            columns = pl.ds(pl.multiple_of(pair * LANES, LANES), LANES)
            pltpu.make_async_copy(feat_ref.at[:, columns], x_buf.at[y * PAIRS + pair, 0, my_rows], x_in).start()
        return carry

    lax.fori_loop(0, PAIRS // 8, stage, 0)
    w_copy.wait()
    pl.semaphore_wait(barrier, len(neighbours))

    def part_copy(layer):
        theirs = pl.ds(pl.multiple_of((1 - core) * MINE * 8, MINE * 8), MINE * 8)
        return pltpu.make_async_remote_copy(
            w_buf.at[layer, theirs], part_buf.at[layer], part_send, part_recv.at[layer],
            device_id=device("c"), device_id_type=MESH,
        )

    part_copies = [part_copy(layer) for layer in range(2)]
    part_copies[0].start()

    def x_copy(number, offset, half, halves, direction):
        source = (y + offset + NY) % NY
        where = x_buf.at[pl.ds(source * PAIRS + half * (PAIRS // 2), halves * (PAIRS // 2)), 0, my_rows]
        return pltpu.make_async_remote_copy(
            where, where, x_send, x_recv.at[min(number, 6)], device_id=device(direction), device_id_type=MESH
        )

    x_copies = {
        "+0": x_copy(0, 0, 0, 1, "y+"),
        "-1": x_copy(1, 0, 1, 1, "y-"),
        "+1": x_copy(2, 0, 1, 1, "y+"),
        "-0": x_copy(3, 0, 0, 1, "y-"),
        "++0": x_copy(4, -1, 0, 1, "y+"),
        "--1": x_copy(5, 1, 1, 1, "y-"),
        "c": x_copy(6, 0, 0, 2, "c"),
        "c+0": x_copy(7, -1, 0, 1, "c"),
        "c-1": x_copy(8, 1, 1, 1, "c"),
        "c+1": x_copy(9, -1, 1, 1, "c"),
        "c-0": x_copy(10, 1, 0, 1, "c"),
        "c++0": x_copy(11, 2, 0, 1, "c"),
        "c--1": x_copy(12, 2, 1, 1, "c"),
    }
    part_copies[1].start()
    mine = x_buf.at[pl.ds(y * PAIRS, PAIRS), 0, my_rows]
    pltpu.make_async_copy(mine, mine, x_in).wait()

    def merge(layer):
        part_copies[layer].wait_recv()
        ours = pl.ds(pl.multiple_of(core * MINE * 8, MINE * 8), MINE * 8)
        own = w_buf[layer, ours, :].astype(jnp.float32).reshape(MINE, 8, LANES)
        other = part_buf[layer].astype(jnp.float32).reshape(MINE, 8, LANES)
        first = core == 0
        both = jnp.concatenate([jnp.where(first, own, other), jnp.where(first, other, own)], axis=1)
        base = ((layer * NX + x) * NZ + z) * MINE
        g_buf[pl.ds(base, MINE)] = both.astype(jnp.bfloat16)

    def flood_copy(number, slot, direction, piece):
        dx, dz, first, count = piece
        layer = CHUNKS[number][0]
        base = ((layer * NX + (x + dx + NX) % NX) * NZ + (z + dz + NZ) % NZ) * MINE + first
        where = g_buf.at[pl.ds(base, count)]
        return pltpu.make_async_remote_copy(
            where, where, flood_send, flood_recv.at[number, slot - 1], device_id=device(direction), device_id_type=MESH
        )

    def flood_issue(number, slot):
        for direction in DIRS:
            for piece in pieces_of(CHUNKS[number], slot, direction):
                flood_copy(number, slot, direction, piece).start()

    def counted(total, number, slot):
        where = g_buf.at[pl.ds(0, total)]
        return pltpu.make_async_remote_copy(
            where, where, flood_send, flood_recv.at[number, slot - 1], device_id=device("x+"), device_id_type=MESH
        )

    def flood_arrived(number, slot):
        counted(sum(tiles_of(CHUNKS[number], slot, direction) for direction in DIRS), number, slot).wait_recv()

    def flood_sent():
        counted(
            sum(
                tiles_of(chunk, slot, direction)
                for chunk in CHUNKS for slot in range(1, SLOTS + 1) for direction in DIRS
            ), 0, 1,
        ).wait_send()

    lane = lax.broadcasted_iota(jnp.int32, (ROWS, LANES), 1)
    low = lane < LANES // 2

    def change_over(panels, first, count):
        def step(at, carry):
            for more in range(8):
                pair = first + at * 8 + more
                panels[pair, 1] = pltpu.roll(panels[pair, 0], LANES // 2, 1)
            return carry

        lax.fori_loop(0, count // 8, step, 0)

    def pair_tile(layer, pair, panels):
        sides = []
        for h in range(2):
            column = (core * MINE + pair) * 2 + h
            tiles = []
            for k in range(0, 8, 2):
                one, two = index_ref[layer, k, column], index_ref[layer, k + 1, column]
                a, b = panels[one >> 1, one & 1], panels[two >> 1, 1 - (two & 1)]
                tiles.append(jnp.where(low, a, b))
            sides.append(jnp.concatenate(tiles, axis=1))
        picked = jnp.concatenate(sides, axis=0)
        w = jnp.concatenate([g_buf[(layer * CHIPS + chip) * MINE + pair] for chip in range(CHIPS)], axis=0)
        total = jnp.dot(picked, w, preferred_element_type=jnp.float32)
        total = jnp.where(low, total[:ROWS], total[ROWS:])
        total = total + bias_ref[layer : layer + 1, pl.ds(pl.multiple_of((core * MINE + pair) * LANES, LANES), LANES)]
        return jnp.maximum(total, 0.0).astype(jnp.bfloat16)

    share = MINE // PARTS

    def y_copy(number, offset, part, direction):
        source = (y + offset + NY) % NY
        where = y_buf.at[pl.ds(source * PAIRS + core * MINE + part * share, share), 0]
        return pltpu.make_async_remote_copy(
            where, where, y_send, y_recv.at[number], device_id=device(direction), device_id_type=MESH
        )

    y_copies = {}
    for part in range(PARTS):
        for number, way in enumerate(("c", "c+", "c-", "cc")):
            y_copies[way, part] = y_copy(number, (0, -1, 1, 2)[number], part, "c")
        y_copies["+", part] = y_copy(4 + part, 0, part, "y+")
        y_copies["-", part] = y_copy(4 + PARTS + part, 0, part, "y-")
        if part < PARTS // 2:
            y_copies["++", part] = y_copy(4 + 2 * PARTS + part, -1, part, "y+")
        else:
            y_copies["--", part] = y_copy(4 + 2 * PARTS + part, 1, part, "y-")

    def y_from_core(number):
        offset = (0, -1, 1, 2)[number]
        where = y_buf.at[pl.ds(0, MINE), 0]
        pltpu.make_async_remote_copy(
            where, where, y_send, y_recv.at[number], device_id=device("c"), device_id_type=MESH
        ).wait_recv()
        change_over(y_buf, (y + offset + NY) % NY * PAIRS + (1 - core) * MINE, MINE)

    def layer_one(part):
        def step(at, carry):
            pair = part * share + at
            tile = pair_tile(0, pair, x_buf)
            y_buf[y * PAIRS + core * MINE + pair, 0] = tile
            y_buf[y * PAIRS + core * MINE + pair, 1] = pltpu.roll(tile, LANES // 2, 1)
            return carry

        lax.fori_loop(0, share, step, 0, unroll=share)

    def layer_two(part):
        def step(at, carry):
            pair = part * share + at
            tile = pair_tile(1, pair, y_buf)
            first = core == 0
            ours = jnp.where(first, tile[:HALF_ROWS], tile[HALF_ROWS:])
            theirs = jnp.where(first, tile[HALF_ROWS:], tile[:HALF_ROWS])
            out_ref[:, pl.ds(pl.multiple_of((core * MINE + pair) * LANES, LANES), LANES)] = ours
            away[:, pl.ds(pl.multiple_of(pair * LANES, LANES), LANES)] = theirs
            return carry

        lax.fori_loop(0, share, step, 0, unroll=share)

    def out_copy(part):
        width = share * LANES
        there = pl.ds(pl.multiple_of((core * MINE + part * share) * LANES, width), width)
        return pltpu.make_async_remote_copy(
            away.at[:, pl.ds(part * width, width)], out_ref.at[:, there], out_send, out_recv,
            device_id=device("c"), device_id_type=MESH,
        )

    out_copies = [out_copy(part) for part in range(PARTS)]

    def x_step(name):
        x_copies[name].wait_recv()
        if name == "+0":
            x_copies["++0"].start()
        if name == "-1":
            x_copies["--1"].start()
        x_copies["c" + name].start()

    def y_step(way, part):
        y_copies[way, part].wait_recv()
        if (way, part < PARTS // 2) in (("+", True), ("-", False)):
            y_copies[way * 2, part].start()
        y_copies["cc" if len(way) == 2 else "c" + way, part].start()
        offset = {"+": -1, "-": 1}.get(way, 2)
        change_over(y_buf, (y + offset + NY) % NY * PAIRS + core * MINE + part * share, share)

    for task in ORDER:
        kind, *rest = task
        if kind == "own":
            for name in ("+0", "-1", "+1", "-0", "c"):
                x_copies[name].start()
        elif kind == "merge":
            merge(*rest)
        elif kind == "flood":
            number, slot = rest
            if slot > 1:
                flood_arrived(number, slot - 1)
            if slot <= SLOTS:
                flood_issue(number, slot)
        elif kind == "x":
            x_step(*rest)
        elif kind == "x_all":
            theirs = pl.ds(pl.multiple_of((1 - core) * HALF_ROWS, HALF_ROWS), HALF_ROWS)
            where = x_buf.at[:, 0, theirs]
            pltpu.make_async_remote_copy(
                where, where, x_send, x_recv.at[6], device_id=device("c"), device_id_type=MESH
            ).wait_recv()
        elif kind == "roll":
            (part,) = rest
            change_over(x_buf, part * PAIRS, PAIRS)
        elif kind == "one":
            (part,) = rest
            layer_one(part)
            for way in ("+", "-", "c"):
                y_copies[way, part].start()
        elif kind == "y":
            y_step(*rest)
        elif kind == "y_in":
            y_from_core(*rest)
        else:
            (part,) = rest
            layer_two(part)
            out_copies[part].start()

    whole = part_buf.at[:]
    pltpu.make_async_remote_copy(
        whole, whole, part_send, part_recv.at[0], device_id=device("c"), device_id_type=MESH
    ).wait_send()
    for buf, send, recv in ((x_buf, x_send, x_recv), (y_buf, y_send, y_recv)):
        moved = buf.at[pl.ds(0, 7 * MINE), 0]
        pltpu.make_async_remote_copy(
            moved, moved, send, recv.at[0], device_id=device("c"), device_id_type=MESH
        ).wait_send()
    flood_sent()
    pltpu.make_async_remote_copy(
        away, away, out_send, out_recv, device_id=device("c"), device_id_type=MESH
    ).wait()


def shards(features, block_rows, weights, biases):
    vmem = pl.BlockSpec(memory_space=pltpu.VMEM)
    anywhere = pl.BlockSpec(memory_space=pl.ANY)
    return pl.pallas_call(
        kernel,
        out_shape=jax.ShapeDtypeStruct((HALF_ROWS, PAIRS * LANES), jnp.bfloat16),
        in_specs=[pl.BlockSpec(memory_space=pltpu.SMEM), anywhere, anywhere, vmem],
        out_specs=vmem,
        scratch_shapes=[
            pltpu.VMEM((NY * PAIRS, 2, ROWS, LANES), jnp.bfloat16),
            pltpu.VMEM((NY * PAIRS, 2, ROWS, LANES), jnp.bfloat16),
            pltpu.VMEM((2 * CHIPS * MINE, 16, LANES), jnp.bfloat16),
            pltpu.VMEM((2, PAIRS * 8, LANES), jnp.bfloat16),
            pltpu.VMEM((2, MINE * 8, LANES), jnp.bfloat16),
            pltpu.VMEM((HALF_ROWS, MINE * LANES), jnp.bfloat16),
            pltpu.SemaphoreType.DMA,
            pltpu.SemaphoreType.DMA((len(CHUNKS), SLOTS)),
            pltpu.SemaphoreType.DMA,
            pltpu.SemaphoreType.DMA((2,)),
            pltpu.SemaphoreType.DMA,
            pltpu.SemaphoreType.DMA((7,)),
            pltpu.SemaphoreType.DMA,
            pltpu.SemaphoreType.DMA((4 + 3 * PARTS,)),
            pltpu.SemaphoreType.DMA,
            pltpu.SemaphoreType.DMA,
            pltpu.SemaphoreType.DMA,
            pltpu.SemaphoreType.DMA,
        ],
        compiler_params=pltpu.CompilerParams(
            collective_id=0, has_side_effects=True, vmem_limit_bytes=56 << 20
        ),
    )(
        block_rows.transpose(0, 2, 1),
        features,
        weights.reshape(2, PAIRS * 8, LANES),
        biases,
    )


def solution(mesh):
    return jax.shard_map(
        shards,
        mesh=mesh,
        in_specs=(
            P("rows", "cols"),
            P(None, "cols", None),
            P(None, "cols", "rows", None),
            P(None, "cols"),
        ),
        out_specs=P("rows", "cols"),
        check_vma=False,
    )
```

```python
import functools

import jax
import jax.numpy as jnp
from jax import lax
from jax.experimental import pallas as pl
from jax.experimental.pallas import tpu as pltpu
from jax.sharding import PartitionSpec as P

MESH = pl.DeviceIdType.MESH
NX, NY, NZ = 4, 4, 8
CHIPS = NX * NZ
PAIRS = 64
MINE = PAIRS // 2
HALF_ROWS = 32
ROWS = 2 * HALF_ROWS
LANES = 128
DIRS = ("x+", "x-", "z+", "z-")
SLOTS = 6

CHUNKS = (
    (0, 0, 3, 5, 1, 3),
    (0, 8, 3, 5, 2, 2),
    (0, 16, 4, 4, 2, 2),
    (0, 24, 3, 5, 1, 3),
    (1, 0, 3, 5, 2, 2),
    (1, 8, 4, 4, 2, 2),
    (1, 16, 3, 5, 1, 3),
    (1, 24, 3, 5, 2, 2),
)
PARTS = 4
ORDER = (
    ("own",), ("merge", 0), ("flood", 0, 1), ("flood", 2, 1), ("flood", 1, 1), ("merge", 1), ("flood", 4, 1),
    ("flood", 3, 1), ("flood", 0, 2), ("flood", 2, 2), ("flood", 1, 2), ("x", "+0"), ("flood", 3, 2), ("x", "-1"),
    ("flood", 0, 3), ("flood", 2, 3), ("flood", 5, 1), ("flood", 1, 3), ("flood", 0, 4), ("flood", 3, 3),
    ("flood", 2, 4), ("flood", 1, 4), ("x", "-0"), ("x", "+1"), ("x", "--1"), ("flood", 0, 5), ("x", "++0"),
    ("flood", 7, 1), ("flood", 3, 4), ("flood", 6, 1), ("x_all",), ("flood", 1, 5), ("flood", 0, 6), ("roll", 0),
    ("flood", 5, 2), ("roll", 2), ("flood", 2, 5), ("roll", 1), ("flood", 4, 2), ("roll", 3), ("flood", 1, 6),
    ("flood", 3, 5), ("flood", 0, 7), ("one", 0), ("flood", 6, 2), ("flood", 2, 6), ("flood", 7, 2), ("flood", 1, 7),
    ("one", 1), ("flood", 3, 6), ("flood", 4, 3), ("flood", 2, 7), ("flood", 6, 3), ("one", 2), ("flood", 5, 3),
    ("flood", 3, 7), ("y", "+", 0), ("flood", 7, 3), ("one", 3), ("flood", 6, 4), ("y", "-", 1), ("flood", 4, 4),
    ("y", "+", 1), ("flood", 5, 4), ("y_in", 0), ("y", "-", 2), ("flood", 7, 4), ("y", "-", 3), ("flood", 6, 5),
    ("flood", 4, 5), ("y", "-", 0), ("y", "+", 2), ("flood", 5, 5), ("flood", 7, 5), ("y", "+", 3), ("y", "++", 0),
    ("y", "--", 2), ("flood", 6, 6), ("flood", 4, 6), ("flood", 5, 6), ("y_in", 2), ("y", "++", 1), ("y", "--", 3),
    ("y_in", 1), ("flood", 7, 6), ("flood", 6, 7), ("y_in", 3), ("flood", 4, 7), ("two", 0), ("flood", 5, 7),
    ("two", 1), ("two", 2), ("flood", 7, 7), ("two", 3),
)


def pieces_of(chunk, slot, direction):
    _, first, n_a, n_b, a_cut, b_cut = chunk
    plus = direction[1] == "+"
    sign = 1 if plus else -1
    a_all, b_all = (first, n_a), (first + n_a, n_b)
    a_part = (first, a_cut) if plus else (first + a_cut, n_a - a_cut)
    b_part = (first + n_a, b_cut) if plus else (first + n_a + b_cut, n_b - b_cut)
    found = []
    if direction[0] == "z":
        columns = ((1, 0, a_all, a_part), (2, 1, a_all, a_part), (2, -1, a_all, a_part), (3, 2, a_all, a_part), (1, 0, b_all, b_part))
        for start, offset, whole, part in columns:
            step = slot - start
            if 0 <= step <= 2:
                found.append((offset, -sign * step, *whole))
            elif step == 3:
                found.append((offset, -sign * step, *part))
    else:
        if slot == 1:
            found.append((0, 0, *a_all))
        elif slot == 2:
            found.append((-sign, 0, *a_part))
        around = {0: (0,), 1: (1, -1), 2: (2, -2), 3: (3, -3), 4: (4,)}
        for far in around.get(slot - 1, ()):
            found.append((0, far, *b_all))
        for far in around.get(slot - 2, ()):
            found.append((-sign, far, *b_part))
    merged = []
    for piece in found:
        if piece[3] == 0:
            continue
        for at, other in enumerate(merged):
            if other[:2] == piece[:2] and other[2] + other[3] == piece[2]:
                merged[at] = (*other[:3], other[3] + piece[3])
                break
        else:
            merged.append(piece)
    return merged


def tiles_of(chunk, slot, direction):
    return sum(piece[3] for piece in pieces_of(chunk, slot, direction))


def kernel(
    index_ref, feat_ref, w_ref, bias_ref, out_ref,
    x_buf, y_buf, g_buf, w_buf, part_buf, away,
    flood_send, flood_recv, part_send, part_recv, x_send, x_recv, y_send, y_recv, out_send, out_recv, x_in, w_in,
):
    row, y = lax.axis_index("rows"), lax.axis_index("cols")
    core = row % 2
    z = (row // 2) % NZ
    x = row // (2 * NZ)

    def device(direction):
        nx, ny, nz, nc = x, y, z, core
        if direction == "c":
            nc = 1 - core
        else:
            step = 1 if direction[1] == "+" else -1
            if direction[0] == "x":
                nx = (x + step + NX) % NX
            elif direction[0] == "y":
                ny = (y + step + NY) % NY
            else:
                nz = (z + step + NZ) % NZ
        return ((nx * NZ + nz) * 2 + nc, ny)

    barrier = pltpu.get_barrier_semaphore()
    neighbours = DIRS + ("y+", "y-", "c")
    for direction in neighbours:
        pl.semaphore_signal(barrier, inc=1, device_id=device(direction), device_id_type=MESH)

    my_rows = pl.ds(pl.multiple_of(core * HALF_ROWS, HALF_ROWS), HALF_ROWS)
    w_copy = pltpu.make_async_copy(w_ref, w_buf, w_in)
    w_copy.start()

    def stage(step, carry):
        for more in range(8):
            pair = step * 8 + more
            columns = pl.ds(pl.multiple_of(pair * LANES, LANES), LANES)
            pltpu.make_async_copy(feat_ref.at[:, columns], x_buf.at[y * PAIRS + pair, 0, my_rows], x_in).start()
        return carry

    lax.fori_loop(0, PAIRS // 8, stage, 0)
    w_copy.wait()
    pl.semaphore_wait(barrier, len(neighbours))

    def part_copy(layer):
        theirs = pl.ds(pl.multiple_of((1 - core) * MINE * 8, MINE * 8), MINE * 8)
        return pltpu.make_async_remote_copy(
            w_buf.at[layer, theirs], part_buf.at[layer], part_send, part_recv.at[layer],
            device_id=device("c"), device_id_type=MESH,
        )

    part_copies = [part_copy(layer) for layer in range(2)]
    part_copies[0].start()

    def x_copy(number, offset, half, halves, direction):
        source = (y + offset + NY) % NY
        where = x_buf.at[pl.ds(source * PAIRS + half * (PAIRS // 2), halves * (PAIRS // 2)), 0, my_rows]
        return pltpu.make_async_remote_copy(
            where, where, x_send, x_recv.at[min(number, 6)], device_id=device(direction), device_id_type=MESH
        )

    x_copies = {
        "+0": x_copy(0, 0, 0, 1, "y+"),
        "-1": x_copy(1, 0, 1, 1, "y-"),
        "+1": x_copy(2, 0, 1, 1, "y+"),
        "-0": x_copy(3, 0, 0, 1, "y-"),
        "++0": x_copy(4, -1, 0, 1, "y+"),
        "--1": x_copy(5, 1, 1, 1, "y-"),
        "c": x_copy(6, 0, 0, 2, "c"),
        "c+0": x_copy(7, -1, 0, 1, "c"),
        "c-1": x_copy(8, 1, 1, 1, "c"),
        "c+1": x_copy(9, -1, 1, 1, "c"),
        "c-0": x_copy(10, 1, 0, 1, "c"),
        "c++0": x_copy(11, 2, 0, 1, "c"),
        "c--1": x_copy(12, 2, 1, 1, "c"),
    }
    part_copies[1].start()
    mine = x_buf.at[pl.ds(y * PAIRS, PAIRS), 0, my_rows]
    pltpu.make_async_copy(mine, mine, x_in).wait()

    def merge(layer):
        part_copies[layer].wait_recv()
        ours = pl.ds(pl.multiple_of(core * MINE * 8, MINE * 8), MINE * 8)
        own = w_buf[layer, ours, :].astype(jnp.float32).reshape(MINE, 8, LANES)
        other = part_buf[layer].astype(jnp.float32).reshape(MINE, 8, LANES)
        first = core == 0
        both = jnp.concatenate([jnp.where(first, own, other), jnp.where(first, other, own)], axis=1)
        base = ((layer * NX + x) * NZ + z) * MINE
        g_buf[pl.ds(base, MINE)] = both.astype(jnp.bfloat16)

    def flood_copy(number, slot, direction, piece):
        dx, dz, first, count = piece
        layer = CHUNKS[number][0]
        base = ((layer * NX + (x + dx + NX) % NX) * NZ + (z + dz + NZ) % NZ) * MINE + first
        where = g_buf.at[pl.ds(base, count)]
        return pltpu.make_async_remote_copy(
            where, where, flood_send, flood_recv.at[number, slot % 2], device_id=device(direction), device_id_type=MESH
        )

    def flood_issue(number, slot):
        for direction in DIRS:
            for piece in pieces_of(CHUNKS[number], slot, direction):
                flood_copy(number, slot, direction, piece).start()

    def counted(total, number, slot):
        where = g_buf.at[pl.ds(0, total)]
        return pltpu.make_async_remote_copy(
            where, where, flood_send, flood_recv.at[number, slot % 2], device_id=device("x+"), device_id_type=MESH
        )

    def flood_arrived(number, slot):
        counted(sum(tiles_of(CHUNKS[number], slot, direction) for direction in DIRS), number, slot).wait_recv()

    def flood_sent():
        counted(
            sum(
                tiles_of(chunk, slot, direction)
                for chunk in CHUNKS for slot in range(1, SLOTS + 1) for direction in DIRS
            ), 0, 1,
        ).wait_send()

    lane = lax.broadcasted_iota(jnp.int32, (ROWS, LANES), 1)
    low = lane < LANES // 2

    def change_over(panels, first, count):
        def step(at, carry):
            for more in range(8):
                pair = first + at * 8 + more
                panels[pair, 1] = pltpu.roll(panels[pair, 0], LANES // 2, 1)
            return carry

        lax.fori_loop(0, count // 8, step, 0)

    def pair_tile(layer, pair, panels):
        sides = []
        for h in range(2):
            column = (core * MINE + pair) * 2 + h
            tiles = []
            for k in range(0, 8, 2):
                one, two = index_ref[layer, k, column], index_ref[layer, k + 1, column]
                a, b = panels[one >> 1, one & 1], panels[two >> 1, 1 - (two & 1)]
                tiles.append(jnp.where(low, a, b))
            sides.append(jnp.concatenate(tiles, axis=1))
        picked = jnp.concatenate(sides, axis=0)
        w = jnp.concatenate([g_buf[(layer * CHIPS + chip) * MINE + pair] for chip in range(CHIPS)], axis=0)
        total = jnp.dot(picked, w, preferred_element_type=jnp.float32)
        total = jnp.where(low, total[:ROWS], total[ROWS:])
        total = total + bias_ref[layer : layer + 1, pl.ds(pl.multiple_of((core * MINE + pair) * LANES, LANES), LANES)]
        return jnp.maximum(total, 0.0).astype(jnp.bfloat16)

    share = MINE // PARTS

    def y_copy(number, offset, part, direction):
        source = (y + offset + NY) % NY
        where = y_buf.at[pl.ds(source * PAIRS + core * MINE + part * share, share), 0]
        return pltpu.make_async_remote_copy(
            where, where, y_send, y_recv.at[number], device_id=device(direction), device_id_type=MESH
        )

    y_copies = {}
    for part in range(PARTS):
        for number, way in enumerate(("c", "c+", "c-", "cc")):
            y_copies[way, part] = y_copy(number, (0, -1, 1, 2)[number], part, "c")
        y_copies["+", part] = y_copy(4 + part, 0, part, "y+")
        y_copies["-", part] = y_copy(4 + PARTS + part, 0, part, "y-")
        if part < PARTS // 2:
            y_copies["++", part] = y_copy(4 + 2 * PARTS + part, -1, part, "y+")
        else:
            y_copies["--", part] = y_copy(4 + 2 * PARTS + part, 1, part, "y-")

    def y_from_core(number):
        offset = (0, -1, 1, 2)[number]
        where = y_buf.at[pl.ds(0, MINE), 0]
        pltpu.make_async_remote_copy(
            where, where, y_send, y_recv.at[number], device_id=device("c"), device_id_type=MESH
        ).wait_recv()
        change_over(y_buf, (y + offset + NY) % NY * PAIRS + (1 - core) * MINE, MINE)

    def layer_one(part):
        def step(at, carry):
            pair = part * share + at
            tile = pair_tile(0, pair, x_buf)
            y_buf[y * PAIRS + core * MINE + pair, 0] = tile
            y_buf[y * PAIRS + core * MINE + pair, 1] = pltpu.roll(tile, LANES // 2, 1)
            return carry

        lax.fori_loop(0, share, step, 0, unroll=share)

    def layer_two(part):
        def step(at, carry):
            pair = part * share + at
            tile = pair_tile(1, pair, y_buf)
            first = core == 0
            ours = jnp.where(first, tile[:HALF_ROWS], tile[HALF_ROWS:])
            theirs = jnp.where(first, tile[HALF_ROWS:], tile[:HALF_ROWS])
            out_ref[:, pl.ds(pl.multiple_of((core * MINE + pair) * LANES, LANES), LANES)] = ours
            away[:, pl.ds(pl.multiple_of(pair * LANES, LANES), LANES)] = theirs
            return carry

        lax.fori_loop(0, share, step, 0, unroll=share)

    def out_copy(part):
        width = share * LANES
        there = pl.ds(pl.multiple_of((core * MINE + part * share) * LANES, width), width)
        return pltpu.make_async_remote_copy(
            away.at[:, pl.ds(part * width, width)], out_ref.at[:, there], out_send, out_recv,
            device_id=device("c"), device_id_type=MESH,
        )

    out_copies = [out_copy(part) for part in range(PARTS)]

    def x_step(name):
        x_copies[name].wait_recv()
        if name == "+0":
            x_copies["++0"].start()
        if name == "-1":
            x_copies["--1"].start()
        x_copies["c" + name].start()

    def y_step(way, part):
        y_copies[way, part].wait_recv()
        if (way, part < PARTS // 2) in (("+", True), ("-", False)):
            y_copies[way * 2, part].start()
        y_copies["cc" if len(way) == 2 else "c" + way, part].start()
        offset = {"+": -1, "-": 1}.get(way, 2)
        change_over(y_buf, (y + offset + NY) % NY * PAIRS + core * MINE + part * share, share)

    for task in ORDER:
        kind, *rest = task
        if kind == "own":
            for name in ("+0", "-1", "+1", "-0", "c"):
                x_copies[name].start()
        elif kind == "merge":
            merge(*rest)
        elif kind == "flood":
            number, slot = rest
            if slot > 1:
                flood_arrived(number, slot - 1)
            if slot <= SLOTS:
                flood_issue(number, slot)
        elif kind == "x":
            x_step(*rest)
        elif kind == "x_all":
            theirs = pl.ds(pl.multiple_of((1 - core) * HALF_ROWS, HALF_ROWS), HALF_ROWS)
            where = x_buf.at[:, 0, theirs]
            pltpu.make_async_remote_copy(
                where, where, x_send, x_recv.at[6], device_id=device("c"), device_id_type=MESH
            ).wait_recv()
        elif kind == "roll":
            (part,) = rest
            change_over(x_buf, part * PAIRS, PAIRS)
        elif kind == "one":
            (part,) = rest
            layer_one(part)
            for way in ("+", "-", "c"):
                y_copies[way, part].start()
        elif kind == "y":
            y_step(*rest)
        elif kind == "y_in":
            y_from_core(*rest)
        else:
            (part,) = rest
            layer_two(part)
            out_copies[part].start()

    whole = part_buf.at[:]
    pltpu.make_async_remote_copy(
        whole, whole, part_send, part_recv.at[0], device_id=device("c"), device_id_type=MESH
    ).wait_send()
    for buf, send, recv in ((x_buf, x_send, x_recv), (y_buf, y_send, y_recv)):
        moved = buf.at[pl.ds(0, 7 * MINE), 0]
        pltpu.make_async_remote_copy(
            moved, moved, send, recv.at[0], device_id=device("c"), device_id_type=MESH
        ).wait_send()
    flood_sent()
    pltpu.make_async_remote_copy(
        away, away, out_send, out_recv, device_id=device("c"), device_id_type=MESH
    ).wait()


def shards(features, block_rows, weights, biases):
    vmem = pl.BlockSpec(memory_space=pltpu.VMEM)
    anywhere = pl.BlockSpec(memory_space=pl.ANY)
    return pl.pallas_call(
        kernel,
        out_shape=jax.ShapeDtypeStruct((HALF_ROWS, PAIRS * LANES), jnp.bfloat16),
        in_specs=[pl.BlockSpec(memory_space=pltpu.SMEM), anywhere, anywhere, vmem],
        out_specs=vmem,
        scratch_shapes=[
            pltpu.VMEM((NY * PAIRS, 2, ROWS, LANES), jnp.bfloat16),
            pltpu.VMEM((NY * PAIRS, 2, ROWS, LANES), jnp.bfloat16),
            pltpu.VMEM((2 * CHIPS * MINE, 16, LANES), jnp.bfloat16),
            pltpu.VMEM((2, PAIRS * 8, LANES), jnp.bfloat16),
            pltpu.VMEM((2, MINE * 8, LANES), jnp.bfloat16),
            pltpu.VMEM((HALF_ROWS, MINE * LANES), jnp.bfloat16),
            pltpu.SemaphoreType.DMA,
            pltpu.SemaphoreType.DMA((len(CHUNKS), 2)),
            pltpu.SemaphoreType.DMA,
            pltpu.SemaphoreType.DMA((2,)),
            pltpu.SemaphoreType.DMA,
            pltpu.SemaphoreType.DMA((7,)),
            pltpu.SemaphoreType.DMA,
            pltpu.SemaphoreType.DMA((4 + 3 * PARTS,)),
            pltpu.SemaphoreType.DMA,
            pltpu.SemaphoreType.DMA,
            pltpu.SemaphoreType.DMA,
            pltpu.SemaphoreType.DMA,
        ],
        compiler_params=pltpu.CompilerParams(
            collective_id=0, has_side_effects=True, vmem_limit_bytes=56 << 20
        ),
    )(
        block_rows.transpose(0, 2, 1),
        features,
        weights.reshape(2, PAIRS * 8, LANES),
        biases,
    )


def solution(mesh):
    return jax.shard_map(
        shards,
        mesh=mesh,
        in_specs=(
            P("rows", "cols"),
            P(None, "cols", None),
            P(None, "cols", "rows", None),
            P(None, "cols"),
        ),
        out_specs=P("rows", "cols"),
        check_vma=False,
    )
```

```python
import functools

import jax
import jax.numpy as jnp
from jax import lax
from jax.experimental import pallas as pl
from jax.experimental.pallas import tpu as pltpu
from jax.sharding import PartitionSpec as P

MESH = pl.DeviceIdType.MESH
NX, NY, NZ = 4, 4, 8
CHIPS = NX * NZ
PAIRS = 64
MINE = PAIRS // 2
HALF_ROWS = 32
ROWS = 2 * HALF_ROWS
LANES = 128
DIRS = ("x+", "x-", "z+", "z-")
SLOTS = 6

CHUNKS = (
    (0, 0, 2, 2, 1, 1),
    (0, 4, 1, 3, 0, 2),
    (0, 8, 3, 5, 2, 2),
    (0, 16, 4, 4, 2, 2),
    (0, 24, 3, 5, 1, 3),
    (1, 0, 3, 5, 2, 2),
    (1, 8, 4, 4, 2, 2),
    (1, 16, 3, 5, 1, 3),
    (1, 24, 1, 3, 1, 1),
    (1, 28, 2, 2, 1, 1),
)
PARTS = 4
ORDER = (
    ("own",), ("merge", 0), ("flood", 0, 1), ("flood", 1, 1), ("flood", 2, 1), ("flood", 4, 1), ("merge", 1),
    ("flood", 3, 1), ("flood", 8, 1), ("flood", 0, 2), ("flood", 1, 2), ("flood", 2, 2), ("flood", 3, 2),
    ("flood", 0, 3), ("flood", 1, 3), ("x", "+0"), ("x", "-1"), ("flood", 2, 3), ("flood", 4, 2), ("flood", 3, 3),
    ("flood", 1, 4), ("flood", 2, 4), ("x", "-0"), ("flood", 0, 4), ("flood", 5, 1), ("flood", 4, 3), ("flood", 8, 2),
    ("flood", 2, 5), ("flood", 1, 5), ("x", "++0"), ("flood", 0, 5), ("x", "+1"), ("x", "--1"), ("flood", 3, 4),
    ("flood", 4, 4), ("flood", 2, 6), ("flood", 9, 1), ("flood", 1, 6), ("x_all",), ("roll", 2), ("flood", 0, 6),
    ("roll", 3), ("flood", 6, 1), ("flood", 7, 1), ("flood", 3, 5), ("flood", 5, 2), ("flood", 4, 5), ("roll", 0),
    ("roll", 1), ("flood", 0, 7), ("flood", 2, 7), ("flood", 1, 7), ("one", 0), ("flood", 6, 2), ("flood", 3, 6),
    ("flood", 7, 2), ("one", 1), ("flood", 5, 3), ("flood", 4, 6), ("flood", 9, 2), ("flood", 6, 3), ("flood", 3, 7),
    ("one", 2), ("flood", 7, 3), ("flood", 8, 3), ("flood", 4, 7), ("one", 3), ("y", "-", 1), ("flood", 9, 3),
    ("y", "+", 1), ("flood", 5, 4), ("flood", 6, 4), ("y", "-", 2), ("flood", 7, 4), ("y_in", 0), ("y", "+", 0),
    ("flood", 9, 4), ("flood", 8, 4), ("y", "-", 3), ("flood", 5, 5), ("flood", 6, 5), ("flood", 7, 5),
    ("flood", 9, 5), ("y", "--", 2), ("flood", 8, 5), ("y", "+", 3), ("y", "+", 2), ("y", "++", 1), ("flood", 5, 6),
    ("flood", 6, 6), ("y", "-", 0), ("y", "--", 3), ("y", "++", 0), ("flood", 7, 6), ("flood", 9, 6), ("y_in", 2),
    ("flood", 8, 6), ("y_in", 1), ("y_in", 3), ("flood", 5, 7), ("two", 0), ("flood", 6, 7), ("two", 1),
    ("flood", 7, 7), ("two", 2), ("flood", 9, 7), ("flood", 8, 7), ("two", 3),
)


def pieces_of(chunk, slot, direction):
    _, first, n_a, n_b, a_cut, b_cut = chunk
    plus = direction[1] == "+"
    sign = 1 if plus else -1
    a_all, b_all = (first, n_a), (first + n_a, n_b)
    a_part = (first, a_cut) if plus else (first + a_cut, n_a - a_cut)
    b_part = (first + n_a, b_cut) if plus else (first + n_a + b_cut, n_b - b_cut)
    found = []
    if direction[0] == "z":
        columns = ((1, 0, a_all, a_part), (2, 1, a_all, a_part), (2, -1, a_all, a_part), (3, 2, a_all, a_part), (1, 0, b_all, b_part))
        for start, offset, whole, part in columns:
            step = slot - start
            if 0 <= step <= 2:
                found.append((offset, -sign * step, *whole))
            elif step == 3:
                found.append((offset, -sign * step, *part))
    else:
        if slot == 1:
            found.append((0, 0, *a_all))
        elif slot == 2:
            found.append((-sign, 0, *a_part))
        around = {0: (0,), 1: (1, -1), 2: (2, -2), 3: (3, -3), 4: (4,)}
        for far in around.get(slot - 1, ()):
            found.append((0, far, *b_all))
        for far in around.get(slot - 2, ()):
            found.append((-sign, far, *b_part))
    merged = []
    for piece in found:
        if piece[3] == 0:
            continue
        for at, other in enumerate(merged):
            if other[:2] == piece[:2] and other[2] + other[3] == piece[2]:
                merged[at] = (*other[:3], other[3] + piece[3])
                break
        else:
            merged.append(piece)
    return merged


def tiles_of(chunk, slot, direction):
    return sum(piece[3] for piece in pieces_of(chunk, slot, direction))


def kernel(
    index_ref, feat_ref, w_ref, bias_ref, out_ref,
    x_buf, y_buf, g_buf, w_buf, part_buf, away,
    flood_send, flood_recv, part_send, part_recv, x_send, x_recv, y_send, y_recv, out_send, out_recv, x_in, w_in,
):
    row, y = lax.axis_index("rows"), lax.axis_index("cols")
    core = row % 2
    z = (row // 2) % NZ
    x = row // (2 * NZ)

    def device(direction):
        nx, ny, nz, nc = x, y, z, core
        if direction == "c":
            nc = 1 - core
        else:
            step = 1 if direction[1] == "+" else -1
            if direction[0] == "x":
                nx = (x + step + NX) % NX
            elif direction[0] == "y":
                ny = (y + step + NY) % NY
            else:
                nz = (z + step + NZ) % NZ
        return ((nx * NZ + nz) * 2 + nc, ny)

    barrier = pltpu.get_barrier_semaphore()
    neighbours = DIRS + ("y+", "y-", "c")
    for direction in neighbours:
        pl.semaphore_signal(barrier, inc=1, device_id=device(direction), device_id_type=MESH)

    my_rows = pl.ds(pl.multiple_of(core * HALF_ROWS, HALF_ROWS), HALF_ROWS)
    w_copy = pltpu.make_async_copy(w_ref, w_buf, w_in)
    w_copy.start()

    def stage(step, carry):
        for more in range(8):
            pair = step * 8 + more
            columns = pl.ds(pl.multiple_of(pair * LANES, LANES), LANES)
            pltpu.make_async_copy(feat_ref.at[:, columns], x_buf.at[y * PAIRS + pair, 0, my_rows], x_in).start()
        return carry

    lax.fori_loop(0, PAIRS // 8, stage, 0)
    w_copy.wait()
    pl.semaphore_wait(barrier, len(neighbours))

    def part_copy(layer):
        theirs = pl.ds(pl.multiple_of((1 - core) * MINE * 8, MINE * 8), MINE * 8)
        return pltpu.make_async_remote_copy(
            w_buf.at[layer, theirs], part_buf.at[layer], part_send, part_recv.at[layer],
            device_id=device("c"), device_id_type=MESH,
        )

    part_copies = [part_copy(layer) for layer in range(2)]
    part_copies[0].start()

    def x_copy(number, offset, half, halves, direction):
        source = (y + offset + NY) % NY
        where = x_buf.at[pl.ds(source * PAIRS + half * (PAIRS // 2), halves * (PAIRS // 2)), 0, my_rows]
        return pltpu.make_async_remote_copy(
            where, where, x_send, x_recv.at[min(number, 6)], device_id=device(direction), device_id_type=MESH
        )

    x_copies = {
        "+0": x_copy(0, 0, 0, 1, "y+"),
        "-1": x_copy(1, 0, 1, 1, "y-"),
        "+1": x_copy(2, 0, 1, 1, "y+"),
        "-0": x_copy(3, 0, 0, 1, "y-"),
        "++0": x_copy(4, -1, 0, 1, "y+"),
        "--1": x_copy(5, 1, 1, 1, "y-"),
        "c": x_copy(6, 0, 0, 2, "c"),
        "c+0": x_copy(7, -1, 0, 1, "c"),
        "c-1": x_copy(8, 1, 1, 1, "c"),
        "c+1": x_copy(9, -1, 1, 1, "c"),
        "c-0": x_copy(10, 1, 0, 1, "c"),
        "c++0": x_copy(11, 2, 0, 1, "c"),
        "c--1": x_copy(12, 2, 1, 1, "c"),
    }
    part_copies[1].start()
    mine = x_buf.at[pl.ds(y * PAIRS, PAIRS), 0, my_rows]
    pltpu.make_async_copy(mine, mine, x_in).wait()

    def merge(layer):
        part_copies[layer].wait_recv()
        ours = pl.ds(pl.multiple_of(core * MINE * 8, MINE * 8), MINE * 8)
        own = w_buf[layer, ours, :].astype(jnp.float32).reshape(MINE, 8, LANES)
        other = part_buf[layer].astype(jnp.float32).reshape(MINE, 8, LANES)
        first = core == 0
        both = jnp.concatenate([jnp.where(first, own, other), jnp.where(first, other, own)], axis=1)
        base = ((layer * NX + x) * NZ + z) * MINE
        g_buf[pl.ds(base, MINE)] = both.astype(jnp.bfloat16)

    def flood_copy(number, slot, direction, piece):
        dx, dz, first, count = piece
        layer = CHUNKS[number][0]
        base = ((layer * NX + (x + dx + NX) % NX) * NZ + (z + dz + NZ) % NZ) * MINE + first
        where = g_buf.at[pl.ds(base, count)]
        return pltpu.make_async_remote_copy(
            where, where, flood_send, flood_recv.at[number, slot % 2], device_id=device(direction), device_id_type=MESH
        )

    def flood_issue(number, slot):
        for direction in DIRS:
            for piece in pieces_of(CHUNKS[number], slot, direction):
                flood_copy(number, slot, direction, piece).start()

    def counted(total, number, slot):
        where = g_buf.at[pl.ds(0, total)]
        return pltpu.make_async_remote_copy(
            where, where, flood_send, flood_recv.at[number, slot % 2], device_id=device("x+"), device_id_type=MESH
        )

    def flood_arrived(number, slot):
        counted(sum(tiles_of(CHUNKS[number], slot, direction) for direction in DIRS), number, slot).wait_recv()

    def flood_sent():
        counted(
            sum(
                tiles_of(chunk, slot, direction)
                for chunk in CHUNKS for slot in range(1, SLOTS + 1) for direction in DIRS
            ), 0, 1,
        ).wait_send()

    lane = lax.broadcasted_iota(jnp.int32, (ROWS, LANES), 1)
    low = lane < LANES // 2

    def change_over(panels, first, count):
        def step(at, carry):
            for more in range(8):
                pair = first + at * 8 + more
                panels[pair, 1] = pltpu.roll(panels[pair, 0], LANES // 2, 1)
            return carry

        lax.fori_loop(0, count // 8, step, 0)

    def pair_tile(layer, pair, panels):
        sides = []
        for h in range(2):
            column = (core * MINE + pair) * 2 + h
            tiles = []
            for k in range(0, 8, 2):
                one, two = index_ref[layer, k, column], index_ref[layer, k + 1, column]
                a, b = panels[one >> 1, one & 1], panels[two >> 1, 1 - (two & 1)]
                tiles.append(jnp.where(low, a, b))
            sides.append(jnp.concatenate(tiles, axis=1))
        picked = jnp.concatenate(sides, axis=0)
        w = jnp.concatenate([g_buf[(layer * CHIPS + chip) * MINE + pair] for chip in range(CHIPS)], axis=0)
        total = jnp.dot(picked, w, preferred_element_type=jnp.float32)
        total = jnp.where(low, total[:ROWS], total[ROWS:])
        total = total + bias_ref[layer : layer + 1, pl.ds(pl.multiple_of((core * MINE + pair) * LANES, LANES), LANES)]
        return jnp.maximum(total, 0.0).astype(jnp.bfloat16)

    share = MINE // PARTS

    def y_copy(number, offset, part, direction):
        source = (y + offset + NY) % NY
        where = y_buf.at[pl.ds(source * PAIRS + core * MINE + part * share, share), 0]
        return pltpu.make_async_remote_copy(
            where, where, y_send, y_recv.at[number], device_id=device(direction), device_id_type=MESH
        )

    y_copies = {}
    for part in range(PARTS):
        for number, way in enumerate(("c", "c+", "c-", "cc")):
            y_copies[way, part] = y_copy(number, (0, -1, 1, 2)[number], part, "c")
        y_copies["+", part] = y_copy(4 + part, 0, part, "y+")
        y_copies["-", part] = y_copy(4 + PARTS + part, 0, part, "y-")
        if part < PARTS // 2:
            y_copies["++", part] = y_copy(4 + 2 * PARTS + part, -1, part, "y+")
        else:
            y_copies["--", part] = y_copy(4 + 2 * PARTS + part, 1, part, "y-")

    def y_from_core(number):
        offset = (0, -1, 1, 2)[number]
        where = y_buf.at[pl.ds(0, MINE), 0]
        pltpu.make_async_remote_copy(
            where, where, y_send, y_recv.at[number], device_id=device("c"), device_id_type=MESH
        ).wait_recv()
        change_over(y_buf, (y + offset + NY) % NY * PAIRS + (1 - core) * MINE, MINE)

    def layer_one(part):
        def step(at, carry):
            pair = part * share + at
            tile = pair_tile(0, pair, x_buf)
            y_buf[y * PAIRS + core * MINE + pair, 0] = tile
            y_buf[y * PAIRS + core * MINE + pair, 1] = pltpu.roll(tile, LANES // 2, 1)
            return carry

        lax.fori_loop(0, share, step, 0, unroll=share)

    def layer_two(part):
        def step(at, carry):
            pair = part * share + at
            tile = pair_tile(1, pair, y_buf)
            first = core == 0
            ours = jnp.where(first, tile[:HALF_ROWS], tile[HALF_ROWS:])
            theirs = jnp.where(first, tile[HALF_ROWS:], tile[:HALF_ROWS])
            out_ref[:, pl.ds(pl.multiple_of((core * MINE + pair) * LANES, LANES), LANES)] = ours
            away[:, pl.ds(pl.multiple_of(pair * LANES, LANES), LANES)] = theirs
            return carry

        lax.fori_loop(0, share, step, 0, unroll=share)

    def out_copy(part):
        width = share * LANES
        there = pl.ds(pl.multiple_of((core * MINE + part * share) * LANES, width), width)
        return pltpu.make_async_remote_copy(
            away.at[:, pl.ds(part * width, width)], out_ref.at[:, there], out_send, out_recv,
            device_id=device("c"), device_id_type=MESH,
        )

    out_copies = [out_copy(part) for part in range(PARTS)]

    def x_step(name):
        x_copies[name].wait_recv()
        if name == "+0":
            x_copies["++0"].start()
        if name == "-1":
            x_copies["--1"].start()
        x_copies["c" + name].start()

    def y_step(way, part):
        y_copies[way, part].wait_recv()
        if (way, part < PARTS // 2) in (("+", True), ("-", False)):
            y_copies[way * 2, part].start()
        y_copies["cc" if len(way) == 2 else "c" + way, part].start()
        offset = {"+": -1, "-": 1}.get(way, 2)
        change_over(y_buf, (y + offset + NY) % NY * PAIRS + core * MINE + part * share, share)

    for task in ORDER:
        kind, *rest = task
        if kind == "own":
            for name in ("+0", "-1", "+1", "-0", "c"):
                x_copies[name].start()
        elif kind == "merge":
            merge(*rest)
        elif kind == "flood":
            number, slot = rest
            if slot > 1:
                flood_arrived(number, slot - 1)
            if slot <= SLOTS:
                flood_issue(number, slot)
        elif kind == "x":
            x_step(*rest)
        elif kind == "x_all":
            theirs = pl.ds(pl.multiple_of((1 - core) * HALF_ROWS, HALF_ROWS), HALF_ROWS)
            where = x_buf.at[:, 0, theirs]
            pltpu.make_async_remote_copy(
                where, where, x_send, x_recv.at[6], device_id=device("c"), device_id_type=MESH
            ).wait_recv()
        elif kind == "roll":
            (part,) = rest
            change_over(x_buf, part * PAIRS, PAIRS)
        elif kind == "one":
            (part,) = rest
            layer_one(part)
            for way in ("+", "-", "c"):
                y_copies[way, part].start()
        elif kind == "y":
            y_step(*rest)
        elif kind == "y_in":
            y_from_core(*rest)
        else:
            (part,) = rest
            layer_two(part)
            out_copies[part].start()

    whole = part_buf.at[:]
    pltpu.make_async_remote_copy(
        whole, whole, part_send, part_recv.at[0], device_id=device("c"), device_id_type=MESH
    ).wait_send()
    for buf, send, recv in ((x_buf, x_send, x_recv), (y_buf, y_send, y_recv)):
        moved = buf.at[pl.ds(0, 7 * MINE), 0]
        pltpu.make_async_remote_copy(
            moved, moved, send, recv.at[0], device_id=device("c"), device_id_type=MESH
        ).wait_send()
    flood_sent()
    pltpu.make_async_remote_copy(
        away, away, out_send, out_recv, device_id=device("c"), device_id_type=MESH
    ).wait()


def shards(features, block_rows, weights, biases):
    vmem = pl.BlockSpec(memory_space=pltpu.VMEM)
    anywhere = pl.BlockSpec(memory_space=pl.ANY)
    return pl.pallas_call(
        kernel,
        out_shape=jax.ShapeDtypeStruct((HALF_ROWS, PAIRS * LANES), jnp.bfloat16),
        in_specs=[pl.BlockSpec(memory_space=pltpu.SMEM), anywhere, anywhere, vmem],
        out_specs=vmem,
        scratch_shapes=[
            pltpu.VMEM((NY * PAIRS, 2, ROWS, LANES), jnp.bfloat16),
            pltpu.VMEM((NY * PAIRS, 2, ROWS, LANES), jnp.bfloat16),
            pltpu.VMEM((2 * CHIPS * MINE, 16, LANES), jnp.bfloat16),
            pltpu.VMEM((2, PAIRS * 8, LANES), jnp.bfloat16),
            pltpu.VMEM((2, MINE * 8, LANES), jnp.bfloat16),
            pltpu.VMEM((HALF_ROWS, MINE * LANES), jnp.bfloat16),
            pltpu.SemaphoreType.DMA,
            pltpu.SemaphoreType.DMA((len(CHUNKS), 2)),
            pltpu.SemaphoreType.DMA,
            pltpu.SemaphoreType.DMA((2,)),
            pltpu.SemaphoreType.DMA,
            pltpu.SemaphoreType.DMA((7,)),
            pltpu.SemaphoreType.DMA,
            pltpu.SemaphoreType.DMA((4 + 3 * PARTS,)),
            pltpu.SemaphoreType.DMA,
            pltpu.SemaphoreType.DMA,
            pltpu.SemaphoreType.DMA,
            pltpu.SemaphoreType.DMA,
        ],
        compiler_params=pltpu.CompilerParams(
            collective_id=0, has_side_effects=True, vmem_limit_bytes=56 << 20
        ),
    )(
        block_rows.transpose(0, 2, 1),
        features,
        weights.reshape(2, PAIRS * 8, LANES),
        biases,
    )


def solution(mesh):
    return jax.shard_map(
        shards,
        mesh=mesh,
        in_specs=(
            P("rows", "cols"),
            P(None, "cols", None),
            P(None, "cols", "rows", None),
            P(None, "cols"),
        ),
        out_specs=P("rows", "cols"),
        check_vma=False,
    )
```

```python
import functools

import jax
import jax.numpy as jnp
from jax import lax
from jax.experimental import pallas as pl
from jax.experimental.pallas import tpu as pltpu
from jax.sharding import PartitionSpec as P

MESH = pl.DeviceIdType.MESH
NX, NY, NZ = 4, 4, 8
CHIPS = NX * NZ
PAIRS = 64
MINE = PAIRS // 2
HALF_ROWS = 32
ROWS = 2 * HALF_ROWS
LANES = 128
DIRS = ("x+", "x-", "z+", "z-")
SLOTS = 6

CHUNKS = (
    (0, 0, 2, 2, 1, 1),
    (0, 4, 1, 3, 0, 2),
    (0, 8, 3, 5, 2, 2),
    (0, 16, 4, 4, 2, 2),
    (0, 24, 3, 5, 1, 3),
    (1, 0, 3, 5, 2, 2),
    (1, 8, 4, 4, 2, 2),
    (1, 16, 3, 5, 1, 3),
    (1, 24, 1, 3, 1, 1),
    (1, 28, 2, 2, 1, 1),
)
PARTS = 4
ORDER = (
    ("own",), ("weights", 0), ("flood", 0, 1), ("flood", 1, 1), ("flood", 2, 1), ("flood", 4, 1), ("weights", 1),
    ("flood", 3, 1), ("flood", 8, 1), ("flood", 0, 2), ("flood", 1, 2), ("flood", 2, 2), ("flood", 3, 2),
    ("flood", 0, 3), ("flood", 1, 3), ("x", "+0"), ("x", "-1"), ("flood", 2, 3), ("flood", 4, 2), ("flood", 3, 3),
    ("flood", 1, 4), ("flood", 2, 4), ("x", "-0"), ("flood", 0, 4), ("flood", 5, 1), ("flood", 4, 3), ("flood", 8, 2),
    ("flood", 2, 5), ("flood", 1, 5), ("x", "++0"), ("flood", 0, 5), ("x", "+1"), ("x", "--1"), ("flood", 3, 4),
    ("flood", 4, 4), ("flood", 2, 6), ("flood", 9, 1), ("flood", 1, 6), ("x_all",), ("roll", 2), ("flood", 0, 6),
    ("roll", 3), ("flood", 6, 1), ("flood", 7, 1), ("flood", 3, 5), ("flood", 5, 2), ("flood", 4, 5), ("roll", 0),
    ("roll", 1), ("flood", 0, 7), ("flood", 2, 7), ("flood", 1, 7), ("one", 0), ("flood", 6, 2), ("flood", 3, 6),
    ("flood", 7, 2), ("one", 1), ("flood", 5, 3), ("flood", 4, 6), ("flood", 9, 2), ("flood", 6, 3), ("flood", 3, 7),
    ("one", 2), ("flood", 7, 3), ("flood", 8, 3), ("flood", 4, 7), ("one", 3), ("y", "-", 1), ("flood", 9, 3),
    ("y", "+", 1), ("flood", 5, 4), ("flood", 6, 4), ("y", "-", 2), ("flood", 7, 4), ("y_in", 0), ("y", "+", 0),
    ("flood", 9, 4), ("flood", 8, 4), ("y", "-", 3), ("flood", 5, 5), ("flood", 6, 5), ("flood", 7, 5),
    ("flood", 9, 5), ("y", "--", 2), ("flood", 8, 5), ("y", "+", 3), ("y", "+", 2), ("y", "++", 1), ("flood", 5, 6),
    ("flood", 6, 6), ("y", "-", 0), ("y", "--", 3), ("y", "++", 0), ("flood", 7, 6), ("flood", 9, 6), ("y_in", 2),
    ("flood", 8, 6), ("y_in", 1), ("y_in", 3), ("flood", 5, 7), ("two", 0), ("flood", 6, 7), ("two", 1),
    ("flood", 7, 7), ("two", 2), ("flood", 9, 7), ("flood", 8, 7), ("two", 3),
)


def pieces_of(chunk, slot, direction):
    _, first, n_a, n_b, a_cut, b_cut = chunk
    plus = direction[1] == "+"
    sign = 1 if plus else -1
    a_all, b_all = (first, n_a), (first + n_a, n_b)
    a_part = (first, a_cut) if plus else (first + a_cut, n_a - a_cut)
    b_part = (first + n_a, b_cut) if plus else (first + n_a + b_cut, n_b - b_cut)
    found = []
    if direction[0] == "z":
        columns = ((1, 0, a_all, a_part), (2, 1, a_all, a_part), (2, -1, a_all, a_part), (3, 2, a_all, a_part), (1, 0, b_all, b_part))
        for start, offset, whole, part in columns:
            step = slot - start
            if 0 <= step <= 2:
                found.append((offset, -sign * step, *whole))
            elif step == 3:
                found.append((offset, -sign * step, *part))
    else:
        if slot == 1:
            found.append((0, 0, *a_all))
        elif slot == 2:
            found.append((-sign, 0, *a_part))
        around = {0: (0,), 1: (1, -1), 2: (2, -2), 3: (3, -3), 4: (4,)}
        for far in around.get(slot - 1, ()):
            found.append((0, far, *b_all))
        for far in around.get(slot - 2, ()):
            found.append((-sign, far, *b_part))
    merged = []
    for piece in found:
        if piece[3] == 0:
            continue
        for at, other in enumerate(merged):
            if other[:2] == piece[:2] and other[2] + other[3] == piece[2]:
                merged[at] = (*other[:3], other[3] + piece[3])
                break
        else:
            merged.append(piece)
    return merged


def tiles_of(chunk, slot, direction):
    return sum(piece[3] for piece in pieces_of(chunk, slot, direction))


def kernel(
    index_ref, feat_ref, w_ref, bias_ref, out_ref,
    x_buf, y_buf, g_buf, w_buf, part_buf, away,
    flood_send, flood_recv, part_send, part_recv, x_send, x_recv, y_send, y_recv, out_send, out_recv, x_in, w_in,
):
    row, y = lax.axis_index("rows"), lax.axis_index("cols")
    core = row % 2
    z = (row // 2) % NZ
    x = row // (2 * NZ)

    def device(direction):
        nx, ny, nz, nc = x, y, z, core
        if direction == "c":
            nc = 1 - core
        else:
            step = 1 if direction[1] == "+" else -1
            if direction[0] == "x":
                nx = (x + step + NX) % NX
            elif direction[0] == "y":
                ny = (y + step + NY) % NY
            else:
                nz = (z + step + NZ) % NZ
        return ((nx * NZ + nz) * 2 + nc, ny)

    barrier = pltpu.get_barrier_semaphore()
    neighbours = DIRS + ("y+", "y-", "c")
    for direction in neighbours:
        pl.semaphore_signal(barrier, inc=1, device_id=device(direction), device_id_type=MESH)

    my_rows = pl.ds(pl.multiple_of(core * HALF_ROWS, HALF_ROWS), HALF_ROWS)
    w_copy = pltpu.make_async_copy(w_ref, w_buf, w_in)
    w_copy.start()

    def stage(step, carry):
        for more in range(8):
            pair = step * 8 + more
            columns = pl.ds(pl.multiple_of(pair * LANES, LANES), LANES)
            pltpu.make_async_copy(feat_ref.at[:, columns], x_buf.at[y * PAIRS + pair, 0, my_rows], x_in).start()
        return carry

    lax.fori_loop(0, PAIRS // 8, stage, 0)
    w_copy.wait()
    pl.semaphore_wait(barrier, len(neighbours))

    def part_copy(layer):
        theirs = pl.ds(pl.multiple_of((1 - core) * MINE * 8, MINE * 8), MINE * 8)
        return pltpu.make_async_remote_copy(
            w_buf.at[layer, theirs], part_buf.at[layer], part_send, part_recv.at[layer],
            device_id=device("c"), device_id_type=MESH,
        )

    part_copies = [part_copy(layer) for layer in range(2)]
    part_copies[0].start()

    def x_copy(number, offset, half, halves, direction):
        source = (y + offset + NY) % NY
        where = x_buf.at[pl.ds(source * PAIRS + half * (PAIRS // 2), halves * (PAIRS // 2)), 0, my_rows]
        return pltpu.make_async_remote_copy(
            where, where, x_send, x_recv.at[min(number, 6)], device_id=device(direction), device_id_type=MESH
        )

    x_copies = {
        "+0": x_copy(0, 0, 0, 1, "y+"),
        "-1": x_copy(1, 0, 1, 1, "y-"),
        "+1": x_copy(2, 0, 1, 1, "y+"),
        "-0": x_copy(3, 0, 0, 1, "y-"),
        "++0": x_copy(4, -1, 0, 1, "y+"),
        "--1": x_copy(5, 1, 1, 1, "y-"),
        "c": x_copy(6, 0, 0, 2, "c"),
        "c+0": x_copy(7, -1, 0, 1, "c"),
        "c-1": x_copy(8, 1, 1, 1, "c"),
        "c+1": x_copy(9, -1, 1, 1, "c"),
        "c-0": x_copy(10, 1, 0, 1, "c"),
        "c++0": x_copy(11, 2, 0, 1, "c"),
        "c--1": x_copy(12, 2, 1, 1, "c"),
    }
    part_copies[1].start()
    mine = x_buf.at[pl.ds(y * PAIRS, PAIRS), 0, my_rows]
    pltpu.make_async_copy(mine, mine, x_in).wait()

    def merge(number):
        layer, start, n_a, n_b, *_ = CHUNKS[number]
        count = n_a + n_b
        ours = pl.ds(pl.multiple_of((core * MINE + start) * 8, 32), count * 8)
        own = w_buf[layer, ours, :].astype(jnp.float32).reshape(count, 8, LANES)
        other = part_buf[layer, start * 8 : (start + count) * 8, :].astype(jnp.float32).reshape(count, 8, LANES)
        first = core == 0
        both = jnp.concatenate([jnp.where(first, own, other), jnp.where(first, other, own)], axis=1)
        base = ((layer * NX + x) * NZ + z) * MINE + start
        g_buf[pl.ds(base, count)] = both.astype(jnp.bfloat16)

    def flood_copy(number, slot, direction, piece):
        dx, dz, first, count = piece
        layer = CHUNKS[number][0]
        base = ((layer * NX + (x + dx + NX) % NX) * NZ + (z + dz + NZ) % NZ) * MINE + first
        where = g_buf.at[pl.ds(base, count)]
        return pltpu.make_async_remote_copy(
            where, where, flood_send, flood_recv.at[number, slot % 2], device_id=device(direction), device_id_type=MESH
        )

    def flood_issue(number, slot):
        for direction in DIRS:
            for piece in pieces_of(CHUNKS[number], slot, direction):
                flood_copy(number, slot, direction, piece).start()

    def counted(total, number, slot):
        where = g_buf.at[pl.ds(0, total)]
        return pltpu.make_async_remote_copy(
            where, where, flood_send, flood_recv.at[number, slot % 2], device_id=device("x+"), device_id_type=MESH
        )

    def flood_arrived(number, slot):
        counted(sum(tiles_of(CHUNKS[number], slot, direction) for direction in DIRS), number, slot).wait_recv()

    def flood_sent():
        counted(
            sum(
                tiles_of(chunk, slot, direction)
                for chunk in CHUNKS for slot in range(1, SLOTS + 1) for direction in DIRS
            ), 0, 1,
        ).wait_send()

    lane = lax.broadcasted_iota(jnp.int32, (ROWS, LANES), 1)
    low = lane < LANES // 2

    def change_over(panels, first, count):
        def step(at, carry):
            for more in range(8):
                pair = first + at * 8 + more
                panels[pair, 1] = pltpu.roll(panels[pair, 0], LANES // 2, 1)
            return carry

        lax.fori_loop(0, count // 8, step, 0)

    def pair_tile(layer, pair, panels):
        sides = []
        for h in range(2):
            column = (core * MINE + pair) * 2 + h
            tiles = []
            for k in range(0, 8, 2):
                one, two = index_ref[layer, k, column], index_ref[layer, k + 1, column]
                a, b = panels[one >> 1, one & 1], panels[two >> 1, 1 - (two & 1)]
                tiles.append(jnp.where(low, a, b))
            sides.append(jnp.concatenate(tiles, axis=1))
        picked = jnp.concatenate(sides, axis=0)
        w = jnp.concatenate([g_buf[(layer * CHIPS + chip) * MINE + pair] for chip in range(CHIPS)], axis=0)
        total = jnp.dot(picked, w, preferred_element_type=jnp.float32)
        total = jnp.where(low, total[:ROWS], total[ROWS:])
        total = total + bias_ref[layer : layer + 1, pl.ds(pl.multiple_of((core * MINE + pair) * LANES, LANES), LANES)]
        return jnp.maximum(total, 0.0).astype(jnp.bfloat16)

    share = MINE // PARTS

    def y_copy(number, offset, part, direction):
        source = (y + offset + NY) % NY
        where = y_buf.at[pl.ds(source * PAIRS + core * MINE + part * share, share), 0]
        return pltpu.make_async_remote_copy(
            where, where, y_send, y_recv.at[number], device_id=device(direction), device_id_type=MESH
        )

    y_copies = {}
    for part in range(PARTS):
        for number, way in enumerate(("c", "c+", "c-", "cc")):
            y_copies[way, part] = y_copy(number, (0, -1, 1, 2)[number], part, "c")
        y_copies["+", part] = y_copy(4 + part, 0, part, "y+")
        y_copies["-", part] = y_copy(4 + PARTS + part, 0, part, "y-")
        if part < PARTS // 2:
            y_copies["++", part] = y_copy(4 + 2 * PARTS + part, -1, part, "y+")
        else:
            y_copies["--", part] = y_copy(4 + 2 * PARTS + part, 1, part, "y-")

    def y_from_core(number):
        offset = (0, -1, 1, 2)[number]
        where = y_buf.at[pl.ds(0, MINE), 0]
        pltpu.make_async_remote_copy(
            where, where, y_send, y_recv.at[number], device_id=device("c"), device_id_type=MESH
        ).wait_recv()
        change_over(y_buf, (y + offset + NY) % NY * PAIRS + (1 - core) * MINE, MINE)

    def layer_one(part):
        def step(at, carry):
            pair = part * share + at
            tile = pair_tile(0, pair, x_buf)
            y_buf[y * PAIRS + core * MINE + pair, 0] = tile
            y_buf[y * PAIRS + core * MINE + pair, 1] = pltpu.roll(tile, LANES // 2, 1)
            return carry

        lax.fori_loop(0, share, step, 0, unroll=share)

    def layer_two(part):
        def step(at, carry):
            pair = part * share + at
            tile = pair_tile(1, pair, y_buf)
            first = core == 0
            ours = jnp.where(first, tile[:HALF_ROWS], tile[HALF_ROWS:])
            theirs = jnp.where(first, tile[HALF_ROWS:], tile[:HALF_ROWS])
            out_ref[:, pl.ds(pl.multiple_of((core * MINE + pair) * LANES, LANES), LANES)] = ours
            away[:, pl.ds(pl.multiple_of(pair * LANES, LANES), LANES)] = theirs
            return carry

        lax.fori_loop(0, share, step, 0, unroll=share)

    def out_copy(part):
        width = share * LANES
        there = pl.ds(pl.multiple_of((core * MINE + part * share) * LANES, width), width)
        return pltpu.make_async_remote_copy(
            away.at[:, pl.ds(part * width, width)], out_ref.at[:, there], out_send, out_recv,
            device_id=device("c"), device_id_type=MESH,
        )

    out_copies = [out_copy(part) for part in range(PARTS)]

    def x_step(name):
        x_copies[name].wait_recv()
        if name == "+0":
            x_copies["++0"].start()
        if name == "-1":
            x_copies["--1"].start()
        x_copies["c" + name].start()

    def y_step(way, part):
        y_copies[way, part].wait_recv()
        if (way, part < PARTS // 2) in (("+", True), ("-", False)):
            y_copies[way * 2, part].start()
        y_copies["cc" if len(way) == 2 else "c" + way, part].start()
        offset = {"+": -1, "-": 1}.get(way, 2)
        change_over(y_buf, (y + offset + NY) % NY * PAIRS + core * MINE + part * share, share)

    for task in ORDER:
        kind, *rest = task
        if kind == "own":
            for name in ("+0", "-1", "+1", "-0", "c"):
                x_copies[name].start()
        elif kind == "weights":
            part_copies[rest[0]].wait_recv()
        elif kind == "flood":
            number, slot = rest
            if slot > 1:
                flood_arrived(number, slot - 1)
            else:
                merge(number)
            if slot <= SLOTS:
                flood_issue(number, slot)
        elif kind == "x":
            x_step(*rest)
        elif kind == "x_all":
            theirs = pl.ds(pl.multiple_of((1 - core) * HALF_ROWS, HALF_ROWS), HALF_ROWS)
            where = x_buf.at[:, 0, theirs]
            pltpu.make_async_remote_copy(
                where, where, x_send, x_recv.at[6], device_id=device("c"), device_id_type=MESH
            ).wait_recv()
        elif kind == "roll":
            (part,) = rest
            change_over(x_buf, part * PAIRS, PAIRS)
        elif kind == "one":
            (part,) = rest
            layer_one(part)
            for way in ("+", "-", "c"):
                y_copies[way, part].start()
        elif kind == "y":
            y_step(*rest)
        elif kind == "y_in":
            y_from_core(*rest)
        else:
            (part,) = rest
            layer_two(part)
            out_copies[part].start()

    whole = part_buf.at[:]
    pltpu.make_async_remote_copy(
        whole, whole, part_send, part_recv.at[0], device_id=device("c"), device_id_type=MESH
    ).wait_send()
    for buf, send, recv in ((x_buf, x_send, x_recv), (y_buf, y_send, y_recv)):
        moved = buf.at[pl.ds(0, 7 * MINE), 0]
        pltpu.make_async_remote_copy(
            moved, moved, send, recv.at[0], device_id=device("c"), device_id_type=MESH
        ).wait_send()
    flood_sent()
    pltpu.make_async_remote_copy(
        away, away, out_send, out_recv, device_id=device("c"), device_id_type=MESH
    ).wait()


def shards(features, block_rows, weights, biases):
    vmem = pl.BlockSpec(memory_space=pltpu.VMEM)
    anywhere = pl.BlockSpec(memory_space=pl.ANY)
    return pl.pallas_call(
        kernel,
        out_shape=jax.ShapeDtypeStruct((HALF_ROWS, PAIRS * LANES), jnp.bfloat16),
        in_specs=[pl.BlockSpec(memory_space=pltpu.SMEM), anywhere, anywhere, vmem],
        out_specs=vmem,
        scratch_shapes=[
            pltpu.VMEM((NY * PAIRS, 2, ROWS, LANES), jnp.bfloat16),
            pltpu.VMEM((NY * PAIRS, 2, ROWS, LANES), jnp.bfloat16),
            pltpu.VMEM((2 * CHIPS * MINE, 16, LANES), jnp.bfloat16),
            pltpu.VMEM((2, PAIRS * 8, LANES), jnp.bfloat16),
            pltpu.VMEM((2, MINE * 8, LANES), jnp.bfloat16),
            pltpu.VMEM((HALF_ROWS, MINE * LANES), jnp.bfloat16),
            pltpu.SemaphoreType.DMA,
            pltpu.SemaphoreType.DMA((len(CHUNKS), 2)),
            pltpu.SemaphoreType.DMA,
            pltpu.SemaphoreType.DMA((2,)),
            pltpu.SemaphoreType.DMA,
            pltpu.SemaphoreType.DMA((7,)),
            pltpu.SemaphoreType.DMA,
            pltpu.SemaphoreType.DMA((4 + 3 * PARTS,)),
            pltpu.SemaphoreType.DMA,
            pltpu.SemaphoreType.DMA,
            pltpu.SemaphoreType.DMA,
            pltpu.SemaphoreType.DMA,
        ],
        compiler_params=pltpu.CompilerParams(
            collective_id=0, has_side_effects=True, vmem_limit_bytes=56 << 20
        ),
    )(
        block_rows.transpose(0, 2, 1),
        features,
        weights.reshape(2, PAIRS * 8, LANES),
        biases,
    )


def solution(mesh):
    return jax.shard_map(
        shards,
        mesh=mesh,
        in_specs=(
            P("rows", "cols"),
            P(None, "cols", None),
            P(None, "cols", "rows", None),
            P(None, "cols"),
        ),
        out_specs=P("rows", "cols"),
        check_vma=False,
    )
```

```python
import functools

import jax
import jax.numpy as jnp
from jax import lax
from jax.experimental import pallas as pl
from jax.experimental.pallas import tpu as pltpu
from jax.sharding import PartitionSpec as P

MESH = pl.DeviceIdType.MESH
NX, NY, NZ = 4, 4, 8
CHIPS = NX * NZ
PAIRS = 64
MINE = PAIRS // 2
HALF_ROWS = 32
ROWS = 2 * HALF_ROWS
LANES = 128
DIRS = ("x+", "x-", "z+", "z-")
SLOTS = 6

CHUNKS = (
    (0, 0, 2, 2, 1, 1),
    (0, 4, 1, 3, 0, 2),
    (0, 8, 3, 5, 2, 2),
    (0, 16, 4, 4, 2, 2),
    (0, 24, 3, 5, 1, 3),
    (1, 0, 3, 5, 2, 2),
    (1, 8, 4, 4, 2, 2),
    (1, 16, 3, 5, 1, 3),
    (1, 24, 1, 3, 1, 1),
    (1, 28, 2, 2, 1, 1),
)
PARTS = 4
ORDER = (
    ("merge", 0), ("flood", 0, 1), ("own",), ("flood", 1, 1), ("flood", 2, 1), ("flood", 4, 1), ("merge", 1),
    ("flood", 3, 1), ("flood", 8, 1), ("flood", 0, 2), ("flood", 1, 2), ("flood", 2, 2), ("flood", 3, 2),
    ("flood", 0, 3), ("flood", 1, 3), ("x", "+0"), ("x", "-1"), ("flood", 2, 3), ("flood", 4, 2), ("flood", 3, 3),
    ("flood", 1, 4), ("flood", 2, 4), ("x", "-0"), ("flood", 0, 4), ("flood", 5, 1), ("flood", 4, 3), ("flood", 8, 2),
    ("flood", 2, 5), ("flood", 1, 5), ("x", "++0"), ("flood", 0, 5), ("x", "+1"), ("x", "--1"), ("flood", 3, 4),
    ("flood", 4, 4), ("flood", 2, 6), ("flood", 9, 1), ("flood", 1, 6), ("x_all",), ("roll", 2), ("flood", 0, 6),
    ("roll", 3), ("flood", 6, 1), ("flood", 7, 1), ("flood", 3, 5), ("flood", 5, 2), ("flood", 4, 5), ("roll", 0),
    ("roll", 1), ("flood", 0, 7), ("flood", 2, 7), ("flood", 1, 7), ("one", 0), ("flood", 6, 2), ("flood", 3, 6),
    ("flood", 7, 2), ("one", 1), ("flood", 5, 3), ("flood", 4, 6), ("flood", 9, 2), ("flood", 6, 3), ("flood", 3, 7),
    ("one", 2), ("flood", 7, 3), ("flood", 8, 3), ("flood", 4, 7), ("one", 3), ("y", "-", 1), ("flood", 9, 3),
    ("y", "+", 1), ("flood", 5, 4), ("flood", 6, 4), ("y", "-", 2), ("flood", 7, 4), ("y_in", 0), ("y", "+", 0),
    ("flood", 9, 4), ("flood", 8, 4), ("y", "-", 3), ("flood", 5, 5), ("flood", 6, 5), ("flood", 7, 5),
    ("flood", 9, 5), ("y", "--", 2), ("flood", 8, 5), ("y", "+", 3), ("y", "+", 2), ("y", "++", 1), ("flood", 5, 6),
    ("flood", 6, 6), ("y", "-", 0), ("y", "--", 3), ("y", "++", 0), ("flood", 7, 6), ("flood", 9, 6), ("y_in", 2),
    ("flood", 8, 6), ("y_in", 1), ("y_in", 3), ("flood", 5, 7), ("two", 0), ("flood", 6, 7), ("two", 1),
    ("flood", 7, 7), ("two", 2), ("flood", 9, 7), ("flood", 8, 7), ("two", 3),
)


def pieces_of(chunk, slot, direction):
    _, first, n_a, n_b, a_cut, b_cut = chunk
    plus = direction[1] == "+"
    sign = 1 if plus else -1
    a_all, b_all = (first, n_a), (first + n_a, n_b)
    a_part = (first, a_cut) if plus else (first + a_cut, n_a - a_cut)
    b_part = (first + n_a, b_cut) if plus else (first + n_a + b_cut, n_b - b_cut)
    found = []
    if direction[0] == "z":
        columns = ((1, 0, a_all, a_part), (2, 1, a_all, a_part), (2, -1, a_all, a_part), (3, 2, a_all, a_part), (1, 0, b_all, b_part))
        for start, offset, whole, part in columns:
            step = slot - start
            if 0 <= step <= 2:
                found.append((offset, -sign * step, *whole))
            elif step == 3:
                found.append((offset, -sign * step, *part))
    else:
        if slot == 1:
            found.append((0, 0, *a_all))
        elif slot == 2:
            found.append((-sign, 0, *a_part))
        around = {0: (0,), 1: (1, -1), 2: (2, -2), 3: (3, -3), 4: (4,)}
        for far in around.get(slot - 1, ()):
            found.append((0, far, *b_all))
        for far in around.get(slot - 2, ()):
            found.append((-sign, far, *b_part))
    merged = []
    for piece in found:
        if piece[3] == 0:
            continue
        for at, other in enumerate(merged):
            if other[:2] == piece[:2] and other[2] + other[3] == piece[2]:
                merged[at] = (*other[:3], other[3] + piece[3])
                break
        else:
            merged.append(piece)
    return merged


def tiles_of(chunk, slot, direction):
    return sum(piece[3] for piece in pieces_of(chunk, slot, direction))


def kernel(
    index_ref, feat_ref, w_ref, bias_ref, out_ref,
    x_buf, y_buf, g_buf, w_buf, part_buf, away,
    flood_send, flood_recv, part_send, part_recv, x_send, x_recv, y_send, y_recv, out_send, out_recv, x_in, w_in,
):
    row, y = lax.axis_index("rows"), lax.axis_index("cols")
    core = row % 2
    z = (row // 2) % NZ
    x = row // (2 * NZ)

    def device(direction):
        nx, ny, nz, nc = x, y, z, core
        if direction == "c":
            nc = 1 - core
        else:
            step = 1 if direction[1] == "+" else -1
            if direction[0] == "x":
                nx = (x + step + NX) % NX
            elif direction[0] == "y":
                ny = (y + step + NY) % NY
            else:
                nz = (z + step + NZ) % NZ
        return ((nx * NZ + nz) * 2 + nc, ny)

    barrier = pltpu.get_barrier_semaphore()
    neighbours = DIRS + ("y+", "y-", "c")
    for direction in neighbours:
        pl.semaphore_signal(barrier, inc=1, device_id=device(direction), device_id_type=MESH)

    my_rows = pl.ds(pl.multiple_of(core * HALF_ROWS, HALF_ROWS), HALF_ROWS)
    w_copy = pltpu.make_async_copy(w_ref, w_buf, w_in)
    w_copy.start()

    def stage(step, carry):
        for more in range(8):
            pair = step * 8 + more
            columns = pl.ds(pl.multiple_of(pair * LANES, LANES), LANES)
            pltpu.make_async_copy(feat_ref.at[:, columns], x_buf.at[y * PAIRS + pair, 0, my_rows], x_in).start()
        return carry

    lax.fori_loop(0, PAIRS // 8, stage, 0)
    w_copy.wait()
    pl.semaphore_wait(barrier, len(neighbours))

    def part_copy(layer):
        theirs = pl.ds(pl.multiple_of((1 - core) * MINE * 8, MINE * 8), MINE * 8)
        return pltpu.make_async_remote_copy(
            w_buf.at[layer, theirs], part_buf.at[layer], part_send, part_recv.at[layer],
            device_id=device("c"), device_id_type=MESH,
        )

    part_copies = [part_copy(layer) for layer in range(2)]
    part_copies[0].start()

    def x_copy(number, offset, half, halves, direction):
        source = (y + offset + NY) % NY
        where = x_buf.at[pl.ds(source * PAIRS + half * (PAIRS // 2), halves * (PAIRS // 2)), 0, my_rows]
        return pltpu.make_async_remote_copy(
            where, where, x_send, x_recv.at[min(number, 6)], device_id=device(direction), device_id_type=MESH
        )

    x_copies = {
        "+0": x_copy(0, 0, 0, 1, "y+"),
        "-1": x_copy(1, 0, 1, 1, "y-"),
        "+1": x_copy(2, 0, 1, 1, "y+"),
        "-0": x_copy(3, 0, 0, 1, "y-"),
        "++0": x_copy(4, -1, 0, 1, "y+"),
        "--1": x_copy(5, 1, 1, 1, "y-"),
        "c": x_copy(6, 0, 0, 2, "c"),
        "c+0": x_copy(7, -1, 0, 1, "c"),
        "c-1": x_copy(8, 1, 1, 1, "c"),
        "c+1": x_copy(9, -1, 1, 1, "c"),
        "c-0": x_copy(10, 1, 0, 1, "c"),
        "c++0": x_copy(11, 2, 0, 1, "c"),
        "c--1": x_copy(12, 2, 1, 1, "c"),
    }
    part_copies[1].start()

    def merge(layer):
        part_copies[layer].wait_recv()
        ours = pl.ds(pl.multiple_of(core * MINE * 8, MINE * 8), MINE * 8)
        own = w_buf[layer, ours, :].astype(jnp.float32).reshape(MINE, 8, LANES)
        other = part_buf[layer].astype(jnp.float32).reshape(MINE, 8, LANES)
        first = core == 0
        both = jnp.concatenate([jnp.where(first, own, other), jnp.where(first, other, own)], axis=1)
        base = ((layer * NX + x) * NZ + z) * MINE
        g_buf[pl.ds(base, MINE)] = both.astype(jnp.bfloat16)

    def flood_copy(number, slot, direction, piece):
        dx, dz, first, count = piece
        layer = CHUNKS[number][0]
        base = ((layer * NX + (x + dx + NX) % NX) * NZ + (z + dz + NZ) % NZ) * MINE + first
        where = g_buf.at[pl.ds(base, count)]
        return pltpu.make_async_remote_copy(
            where, where, flood_send, flood_recv.at[number, slot % 2], device_id=device(direction), device_id_type=MESH
        )

    def flood_issue(number, slot):
        for direction in DIRS:
            for piece in pieces_of(CHUNKS[number], slot, direction):
                flood_copy(number, slot, direction, piece).start()

    def counted(total, number, slot):
        where = g_buf.at[pl.ds(0, total)]
        return pltpu.make_async_remote_copy(
            where, where, flood_send, flood_recv.at[number, slot % 2], device_id=device("x+"), device_id_type=MESH
        )

    def flood_arrived(number, slot):
        counted(sum(tiles_of(CHUNKS[number], slot, direction) for direction in DIRS), number, slot).wait_recv()

    def flood_sent():
        counted(
            sum(
                tiles_of(chunk, slot, direction)
                for chunk in CHUNKS for slot in range(1, SLOTS + 1) for direction in DIRS
            ), 0, 1,
        ).wait_send()

    lane = lax.broadcasted_iota(jnp.int32, (ROWS, LANES), 1)
    low = lane < LANES // 2

    def change_over(panels, first, count):
        def step(at, carry):
            for more in range(8):
                pair = first + at * 8 + more
                panels[pair, 1] = pltpu.roll(panels[pair, 0], LANES // 2, 1)
            return carry

        lax.fori_loop(0, count // 8, step, 0)

    def pair_tile(layer, pair, panels):
        sides = []
        for h in range(2):
            column = (core * MINE + pair) * 2 + h
            tiles = []
            for k in range(0, 8, 2):
                one, two = index_ref[layer, k, column], index_ref[layer, k + 1, column]
                a, b = panels[one >> 1, one & 1], panels[two >> 1, 1 - (two & 1)]
                tiles.append(jnp.where(low, a, b))
            sides.append(jnp.concatenate(tiles, axis=1))
        picked = jnp.concatenate(sides, axis=0)
        w = jnp.concatenate([g_buf[(layer * CHIPS + chip) * MINE + pair] for chip in range(CHIPS)], axis=0)
        total = jnp.dot(picked, w, preferred_element_type=jnp.float32)
        total = jnp.where(low, total[:ROWS], total[ROWS:])
        total = total + bias_ref[layer : layer + 1, pl.ds(pl.multiple_of((core * MINE + pair) * LANES, LANES), LANES)]
        return jnp.maximum(total, 0.0).astype(jnp.bfloat16)

    share = MINE // PARTS

    def y_copy(number, offset, part, direction):
        source = (y + offset + NY) % NY
        where = y_buf.at[pl.ds(source * PAIRS + core * MINE + part * share, share), 0]
        return pltpu.make_async_remote_copy(
            where, where, y_send, y_recv.at[number], device_id=device(direction), device_id_type=MESH
        )

    y_copies = {}
    for part in range(PARTS):
        for number, way in enumerate(("c", "c+", "c-", "cc")):
            y_copies[way, part] = y_copy(number, (0, -1, 1, 2)[number], part, "c")
        y_copies["+", part] = y_copy(4 + part, 0, part, "y+")
        y_copies["-", part] = y_copy(4 + PARTS + part, 0, part, "y-")
        if part < PARTS // 2:
            y_copies["++", part] = y_copy(4 + 2 * PARTS + part, -1, part, "y+")
        else:
            y_copies["--", part] = y_copy(4 + 2 * PARTS + part, 1, part, "y-")

    def y_from_core(number):
        offset = (0, -1, 1, 2)[number]
        where = y_buf.at[pl.ds(0, MINE), 0]
        pltpu.make_async_remote_copy(
            where, where, y_send, y_recv.at[number], device_id=device("c"), device_id_type=MESH
        ).wait_recv()
        change_over(y_buf, (y + offset + NY) % NY * PAIRS + (1 - core) * MINE, MINE)

    def layer_one(part):
        def step(at, carry):
            pair = part * share + at
            tile = pair_tile(0, pair, x_buf)
            y_buf[y * PAIRS + core * MINE + pair, 0] = tile
            y_buf[y * PAIRS + core * MINE + pair, 1] = pltpu.roll(tile, LANES // 2, 1)
            return carry

        lax.fori_loop(0, share, step, 0, unroll=share)

    def layer_two(part):
        def step(at, carry):
            pair = part * share + at
            tile = pair_tile(1, pair, y_buf)
            first = core == 0
            ours = jnp.where(first, tile[:HALF_ROWS], tile[HALF_ROWS:])
            theirs = jnp.where(first, tile[HALF_ROWS:], tile[:HALF_ROWS])
            out_ref[:, pl.ds(pl.multiple_of((core * MINE + pair) * LANES, LANES), LANES)] = ours
            away[:, pl.ds(pl.multiple_of(pair * LANES, LANES), LANES)] = theirs
            return carry

        lax.fori_loop(0, share, step, 0, unroll=share)

    def out_copy(part):
        width = share * LANES
        there = pl.ds(pl.multiple_of((core * MINE + part * share) * LANES, width), width)
        return pltpu.make_async_remote_copy(
            away.at[:, pl.ds(part * width, width)], out_ref.at[:, there], out_send, out_recv,
            device_id=device("c"), device_id_type=MESH,
        )

    out_copies = [out_copy(part) for part in range(PARTS)]

    def x_step(name):
        x_copies[name].wait_recv()
        if name == "+0":
            x_copies["++0"].start()
        if name == "-1":
            x_copies["--1"].start()
        x_copies["c" + name].start()

    def y_step(way, part):
        y_copies[way, part].wait_recv()
        if (way, part < PARTS // 2) in (("+", True), ("-", False)):
            y_copies[way * 2, part].start()
        y_copies["cc" if len(way) == 2 else "c" + way, part].start()
        offset = {"+": -1, "-": 1}.get(way, 2)
        change_over(y_buf, (y + offset + NY) % NY * PAIRS + core * MINE + part * share, share)

    for task in ORDER:
        kind, *rest = task
        if kind == "own":
            mine = x_buf.at[pl.ds(y * PAIRS, PAIRS), 0, my_rows]
            pltpu.make_async_copy(mine, mine, x_in).wait()
            for name in ("+0", "-1", "+1", "-0", "c"):
                x_copies[name].start()
        elif kind == "merge":
            merge(*rest)
        elif kind == "flood":
            number, slot = rest
            if slot > 1:
                flood_arrived(number, slot - 1)
            if slot <= SLOTS:
                flood_issue(number, slot)
        elif kind == "x":
            x_step(*rest)
        elif kind == "x_all":
            theirs = pl.ds(pl.multiple_of((1 - core) * HALF_ROWS, HALF_ROWS), HALF_ROWS)
            where = x_buf.at[:, 0, theirs]
            pltpu.make_async_remote_copy(
                where, where, x_send, x_recv.at[6], device_id=device("c"), device_id_type=MESH
            ).wait_recv()
        elif kind == "roll":
            (part,) = rest
            change_over(x_buf, part * PAIRS, PAIRS)
        elif kind == "one":
            (part,) = rest
            layer_one(part)
            for way in ("+", "-", "c"):
                y_copies[way, part].start()
        elif kind == "y":
            y_step(*rest)
        elif kind == "y_in":
            y_from_core(*rest)
        else:
            (part,) = rest
            layer_two(part)
            out_copies[part].start()

    whole = part_buf.at[:]
    pltpu.make_async_remote_copy(
        whole, whole, part_send, part_recv.at[0], device_id=device("c"), device_id_type=MESH
    ).wait_send()
    for buf, send, recv in ((x_buf, x_send, x_recv), (y_buf, y_send, y_recv)):
        moved = buf.at[pl.ds(0, 7 * MINE), 0]
        pltpu.make_async_remote_copy(
            moved, moved, send, recv.at[0], device_id=device("c"), device_id_type=MESH
        ).wait_send()
    flood_sent()
    pltpu.make_async_remote_copy(
        away, away, out_send, out_recv, device_id=device("c"), device_id_type=MESH
    ).wait()


def shards(features, block_rows, weights, biases):
    vmem = pl.BlockSpec(memory_space=pltpu.VMEM)
    anywhere = pl.BlockSpec(memory_space=pl.ANY)
    return pl.pallas_call(
        kernel,
        out_shape=jax.ShapeDtypeStruct((HALF_ROWS, PAIRS * LANES), jnp.bfloat16),
        in_specs=[pl.BlockSpec(memory_space=pltpu.SMEM), anywhere, anywhere, vmem],
        out_specs=vmem,
        scratch_shapes=[
            pltpu.VMEM((NY * PAIRS, 2, ROWS, LANES), jnp.bfloat16),
            pltpu.VMEM((NY * PAIRS, 2, ROWS, LANES), jnp.bfloat16),
            pltpu.VMEM((2 * CHIPS * MINE, 16, LANES), jnp.bfloat16),
            pltpu.VMEM((2, PAIRS * 8, LANES), jnp.bfloat16),
            pltpu.VMEM((2, MINE * 8, LANES), jnp.bfloat16),
            pltpu.VMEM((HALF_ROWS, MINE * LANES), jnp.bfloat16),
            pltpu.SemaphoreType.DMA,
            pltpu.SemaphoreType.DMA((len(CHUNKS), 2)),
            pltpu.SemaphoreType.DMA,
            pltpu.SemaphoreType.DMA((2,)),
            pltpu.SemaphoreType.DMA,
            pltpu.SemaphoreType.DMA((7,)),
            pltpu.SemaphoreType.DMA,
            pltpu.SemaphoreType.DMA((4 + 3 * PARTS,)),
            pltpu.SemaphoreType.DMA,
            pltpu.SemaphoreType.DMA,
            pltpu.SemaphoreType.DMA,
            pltpu.SemaphoreType.DMA,
        ],
        compiler_params=pltpu.CompilerParams(
            collective_id=0, has_side_effects=True, vmem_limit_bytes=56 << 20
        ),
    )(
        block_rows.transpose(0, 2, 1),
        features,
        weights.reshape(2, PAIRS * 8, LANES),
        biases,
    )


def solution(mesh):
    return jax.shard_map(
        shards,
        mesh=mesh,
        in_specs=(
            P("rows", "cols"),
            P(None, "cols", None),
            P(None, "cols", "rows", None),
            P(None, "cols"),
        ),
        out_specs=P("rows", "cols"),
        check_vma=False,
    )
```
